256 devices in a mesh: space: 8 (over x, y_lo), tm: 32 (over y_hi, z, core).
Axes of the slice: x: 4, y: 4 (y_hi: 2, y_lo: 2; y = y_hi * 2 + y_lo), z: 8, core: 2. Of those that a mesh axis runs over, the one named last changes fastest.
Arguments:
- volume: float32 [32, 32, 128, 128], P('tm', 'space'), may hold values from -6 to 6
- lift_weights: bfloat16 [3, 64, 27], replicated, may hold values from -1.25 to 1.25
- lift_bias: float32 [3, 64], replicated, may hold values from -3 to 3
- mix_weights: bfloat16 [3, 64, 64], replicated, may hold values from -0.75 to 0.75
- out_weights: bfloat16 [3, 64], replicated, may hold values from -0.75 to 0.75
- projector: bfloat16 [2048, 16384], P(None, 'tm'), may hold values from -0.046875 to 0.046875
- measured: float32 [32, 32, 2048], P('tm', 'space'), may hold values from -6 to 6
Outputs:
- updated: float32 [32, 32, 16384], P(None, 'space', 'tm')
The draws below stay inside these ranges and needn't reach their ends.
All inputs are finite; a program needn't handle non-finite values.
Results may differ from the reference program's by a relative error of at most 0.0027.
Values may be sent and summed in bfloat16 or wider, within the bound.
No kernel may reach another device: no remote copies, remote signals or barrier semaphores. Data moves between devices by JAX's collectives and lax.ppermute only.
A program may use at most 64 MiB of HBM per device.

```python
import jax
import jax.numpy as jnp
from jax import lax

X = 128
Y = 128
CH = 64
RAYS = 2048
NT = 32
NZ = 32
PIX = 16384


def shard_levels(key, shape, split, low, top_value):
    level, own = 1.0, jax.random.fold_in(key, 6)
    for position, parts in split:
        steps = jnp.exp(jax.random.uniform(jax.random.fold_in(own, position), (parts,), jnp.float32, low / len(split), top_value / len(split)))
        level = level * jnp.repeat(steps, shape[position] // parts).reshape([-1 if axis == position else 1 for axis in range(len(shape))])
    return level


def gaussian(key, extent, spread, bound, pieces=(), kind=jnp.bfloat16):
    values = jax.random.normal(key, extent, jnp.float32) * spread
    if len(pieces) > 0:
        values = shard_levels(key, extent, pieces, -0.22, 0.18) * values
    return jnp.clip(values, min=-bound, max=bound).astype(kind)


def setup_inputs(seed: int = 0) -> dict:
    arg_keys = jax.random.split(jax.random.key(seed), 8)
    return {
        "volume": gaussian(arg_keys[0], (NT, NZ, X, Y), 1.0, 6.0, ((0, 32), (1, 8)), jnp.float32),
        "lift_weights": gaussian(arg_keys[1], (3, CH, 27), 27 ** -0.5, 1.25),
        "lift_bias": gaussian(arg_keys[2], (3, CH), 0.5, 3.0, (), jnp.float32),
        "mix_weights": gaussian(arg_keys[3], (3, CH, CH), CH ** -0.5, 0.75),
        "out_weights": gaussian(arg_keys[4], (3, CH), CH ** -0.5, 0.75),
        "projector": gaussian(arg_keys[5], (RAYS, PIX), PIX ** -0.5, 0.046875, ((1, 32),)),
        "measured": gaussian(arg_keys[6], (NT, NZ, RAYS), 1.0, 6.0, ((0, 32), (1, 8)), jnp.float32),
    }


def lift_taps(block, planes):
    pads = [(0, 0)] + [(1, 1) if d in planes else (0, 0) for d in (1, 2, 3)]
    padded = jnp.pad(block, pads)
    frames = block.shape[0] - 2
    shape = block.shape
    taps = []
    for dt in range(3):
        for da in range(3):
            for db in range(3):
                start = [dt, 0, 0, 0]
                start[planes[0]] = da
                start[planes[1]] = db
                limit = [dt + frames] + [start[i] + shape[i] for i in (1, 2, 3)]
                taps.append(lax.slice(padded, start, limit))
    return jnp.stack(taps, 0)


def correction(block, planes, which, lift_weights, lift_bias, mix_weights, out_weights):
    taps = lift_taps(block, planes).astype(jnp.float32)
    pre = jnp.einsum("ck,kfpqr->cfpqr", lift_weights[which].astype(jnp.float32), taps)
    pre = pre + lift_bias[which][:, None, None, None, None]
    first = jax.nn.relu(pre).astype(jnp.bfloat16).astype(jnp.float32)
    second = jax.nn.relu(jnp.einsum("cd,dfpqr->cfpqr", mix_weights[which].astype(jnp.float32), first))
    second = second.astype(jnp.bfloat16).astype(jnp.float32)
    return jnp.einsum("c,cfpqr->fpqr", out_weights[which].astype(jnp.float32), second)


def reference(volume, lift_weights, lift_bias, mix_weights, out_weights, projector, measured):
    coarse = volume.astype(jnp.bfloat16)
    padded = jnp.pad(coarse, ((1, 1), (0, 0), (0, 0), (0, 0)))

    def frame(index):
        block = lax.dynamic_slice_in_dim(padded, index, 3, 0)
        total = correction(block, (2, 3), 0, lift_weights, lift_bias, mix_weights, out_weights)
        total = total + correction(block, (3, 1), 1, lift_weights, lift_bias, mix_weights, out_weights)
        total = total + correction(block, (1, 2), 2, lift_weights, lift_bias, mix_weights, out_weights)
        return total[0]

    corrections = lax.map(frame, jnp.arange(NT, dtype=jnp.int32))
    consensus = volume + corrections / 3.0
    rows = consensus.reshape(NT * NZ, X * Y)
    image = rows.astype(jnp.bfloat16)
    predicted = jnp.dot(image, projector.T, preferred_element_type=jnp.float32)
    misfit = (predicted - measured.reshape(NT * NZ, RAYS)).astype(jnp.bfloat16)
    gradient = jnp.dot(misfit, projector, preferred_element_type=jnp.float32)
    return (rows - gradient).reshape(NT, NZ, X * Y)
```

```python
import functools

import jax
import jax.numpy as jnp
from jax import lax
from jax.experimental import pallas as pl
from jax.experimental.pallas import tpu as pltpu
from jax.sharding import Mesh, PartitionSpec as P

F32, BF16 = jnp.float32, jnp.bfloat16
VM = pl.BlockSpec(memory_space=pltpu.VMEM)
SM = pl.BlockSpec(memory_space=pltpu.SMEM)
SWAP = [(0, 1), (1, 0)]


def call(kernel, outs, scratch=(), specs=None, flops=0, nbytes=0, vmem=40):
    return pl.pallas_call(
        kernel,
        out_shape=outs,
        in_specs=specs,
        out_specs=jax.tree.map(lambda _: VM, outs),
        scratch_shapes=list(scratch),
        compiler_params=pltpu.CompilerParams(vmem_limit_bytes=vmem << 20),
        cost_estimate=pl.CostEstimate(flops=flops, bytes_accessed=nbytes, transcendentals=0),
    )


def shaped(shape, dtype):
    return jax.ShapeDtypeStruct(shape, dtype)


def iota(shape, dim):
    return lax.broadcasted_iota(jnp.int32, shape, dim)


def weights_kernel(lift, mix, outw, a1, a2, a3):
    spread = (iota((256, 64), 0) >> 2 == iota((256, 64), 1)).astype(F32).astype(BF16)
    spread_t = (iota((64, 256), 1) >> 2 == iota((64, 256), 0)).astype(F32).astype(BF16)
    taps = (iota((32, 256), 1) >> 3 == iota((32, 256), 0)).astype(F32).astype(BF16)
    row, col = iota((256, 256), 0) & 3, iota((256, 256), 1)
    part = iota((64, 32), 1)
    for k in range(3):
        full = lift[k]
        high = full.astype(BF16).astype(F32)
        mid = (full - high).astype(BF16).astype(F32)
        low = full - high - mid
        split = jnp.where(part == 28, mid, jnp.where(part == 29, low, high)).astype(BF16)
        base = jnp.dot(spread, split, preferred_element_type=F32).astype(BF16)
        base = jnp.dot(base, taps, preferred_element_type=F32)
        for half in range(2):
            a1[k, half * 256 : half * 256 + 256] = jnp.where(
                row + 4 * half == (col & 7), base, 0.0
            ).astype(BF16)
        mixed = jnp.dot(spread, mix[k], preferred_element_type=F32).astype(BF16)
        mixed = jnp.dot(mixed, spread_t, preferred_element_type=F32)
        a2[k] = jnp.where(row == (col & 3), mixed, 0.0).astype(BF16)
        a3[k] = jnp.dot(spread, outw[k], preferred_element_type=F32)


def pack_kernel(vol, out):
    zero = jnp.zeros((1, 128), F32)
    for p in range(32):
        for z in range(4):
            lo, hi = max(4 * p - 1, 0), min(4 * p + 5, 128)
            at = z * 6 + lo - (4 * p - 1)
            out[p, at : at + hi - lo] = vol[z, lo:hi]
            if p == 0:
                out[p, z * 6 : z * 6 + 1] = zero
            if p == 31:
                out[p, z * 6 + 5 : z * 6 + 6] = zero


def turn_kernel(rows, vol, first, last):
    zero = jnp.zeros((8, 128), F32)
    for r in range(24):
        x = rows[pl.ds(r, 32, stride=24), :]
        vol[r, 0:8] = zero
        vol[r, 8:40] = x
        vol[r, 40:48] = zero
        if r < 6:
            first[r] = x.astype(BF16)
        if r >= 18:
            last[r - 18] = x.astype(BF16)


def spread_y(s, pos, v):
    lane = iota(v.shape, 1)
    s[0, pos] = jnp.where(lane == 0, 0.0, pltpu.roll(v, 1, 1))
    s[1, pos] = v
    s[2, pos] = jnp.where(lane == 127, 0.0, pltpu.roll(v, 127, 1))


OFFSETS = (
    [(dt, db, da - 1) for dt in range(3) for da in range(3) for db in range(3)],
    [(dt, da, 6 * (db - 1)) for dt in range(3) for da in range(3) for db in range(3)],
    [(dt, 1, 6 * (da - 1) + db - 1) for dt in range(3) for da in range(3) for db in range(3)],
)


def corrected(s, a1, a2, a3, which, weight, pos, block):
    rows = []
    for dt, dy, step in OFFSETS[which]:
        at = pl.ds(7 + dt + 8 * block, 8)
        rows.append(
            jnp.concatenate([s[dy, pos + step, at, :], s[dy, pos + step + 1, at, :]], axis=1)
        )
    rows.append(jnp.ones((24, 256), F32))
    rows.append(jnp.zeros((16, 256), F32))
    taps = jnp.concatenate(rows, axis=0).astype(BF16)
    first = jnp.dot(a1[weight], taps, preferred_element_type=F32)
    first = jnp.maximum(first, 0.0).astype(BF16)
    w = a3[weight]
    w = jnp.concatenate([w, w], axis=1)
    sums = []
    for half in range(2):
        second = jnp.dot(
            a2[weight], first[half * 256 : half * 256 + 256], preferred_element_type=F32
        )
        second = jnp.maximum(second, 0.0) * w
        total = jnp.sum(second.reshape(32, 8, 256), axis=0)
        sums.append(total + pltpu.roll(total, 4, 0))
    return jnp.where(iota((8, 256), 0) < 4, sums[0], sums[1])


def xy_kernel(vol, a1, a2, a3, out, s):
    def fill(r, carry):
        spread_y(s, r + 6, vol[r])
        return carry

    lax.fori_loop(0, 24, fill, 0)

    def step(i, carry):
        z, x = i // 2, 2 * (i % 2)
        pos = (z + 1) * 6 + 1 + x
        for block in range(4):
            got = corrected(s, a1, a2, a3, 0, 0, pos, block)
            out[z * 4 + x, 8 * block : 8 * block + 8] = got[:, :128]
            out[z * 4 + x + 1, 8 * block : 8 * block + 8] = got[:, 128:]
        return carry

    lax.fori_loop(0, 8, step, 0)


def rest_kernel(core, vol, before, after, xy, a1, a2, a3, cons, mine, other, s):
    def fill(r, carry):
        spread_y(s, r + 6, vol[r])
        return carry

    lax.fori_loop(0, 24, fill, 0)
    edge = jnp.zeros((8, 128), F32)

    def fill_edge(r, carry):
        spread_y(s, r, jnp.concatenate([edge, before[r].astype(F32), edge], axis=0))
        spread_y(s, r + 30, jnp.concatenate([edge, after[r].astype(F32), edge], axis=0))
        return carry

    lax.fori_loop(0, 6, fill_edge, 0)

    def step(i, carry):
        z, x = i // 2, 2 * (i % 2)
        pos = (z + 1) * 6 + 1 + x
        for block in range(4):
            at = slice(8 * block, 8 * block + 8)
            got = corrected(s, a1, a2, a3, 1, 1, pos, block)
            got = got + corrected(s, a1, a2, a3, 2, 2, pos, block)
            for j in range(2):
                total = xy[z * 4 + x + j, at] + got[:, 128 * j : 128 * j + 128]
                here = vol[pos - 6 + j, 8 + 8 * block : 16 + 8 * block]
                cons[z * 4 + x + j, at] = here + total / 3.0
        return carry

    lax.fori_loop(0, 8, step, 0)
    c = core[0]
    for z in range(4):
        for x in range(4):
            at = (slice(16 * z, 16 * z + 16), slice(128 * x, 128 * x + 128))
            even = cons[z * 4 + x, pl.ds(0, 16, stride=2), :].astype(BF16)
            odd = cons[z * 4 + x, pl.ds(1, 16, stride=2), :].astype(BF16)

            @pl.when(c == 0)
            def _():
                mine[at] = even
                other[at] = odd

            @pl.when(c == 1)
            def _():
                mine[at] = odd
                other[at] = even


NT = (((1,), (1,)), ((), ()))


def project_kernel(mine, theirs, own, pair, out, turned):
    for j in range(8):
        rays = slice(256 * j, 256 * j + 256)
        got = lax.dot_general(mine[...], own[rays], NT, preferred_element_type=F32)
        got = got + lax.dot_general(theirs[...], pair[rays], NT, preferred_element_type=F32)
        for z in range(4):
            for n in range(2):
                turned[2 * (j % 4) + n, pl.ds(z * 2 + j // 4, 16, stride=8), :] = got[
                    16 * z : 16 * z + 16, 128 * n : 128 * n + 128
                ]
    for n in range(8):
        lanes = slice(128 * n, 128 * n + 128)
        for t in range(16):
            out[t, :, lanes] = turned[n, 8 * t : 8 * t + 8].astype(BF16)


def misfit_kernel(parts, measured, out):
    total = parts[0].astype(F32)
    for t in range(1, 16):
        total = total + parts[t].astype(F32)
    misfit = (total - measured[...]).astype(BF16)
    for t in range(16):
        out[t] = misfit


def gradient_kernel(misfit, own, pair, near, far, turned, rows):
    for n in range(8):
        for t in range(16):
            turned[n, 8 * t : 8 * t + 8] = misfit[t, :, 128 * n : 128 * n + 128].astype(F32)
    for z in range(4):
        for half in range(2):
            for n in range(8):
                rows[16 * z : 16 * z + 16, 1024 * half + 128 * n : 1024 * half + 128 * n + 128] = (
                    turned[n, pl.ds(z * 2 + half, 16, stride=8), :].astype(BF16)
                )
    left = rows[...]
    far[...] = jnp.dot(left, pair[...], preferred_element_type=F32)
    near[...] = jnp.dot(left, own[...], preferred_element_type=F32)


def update_kernel(core, cons, near, far, out, turned):
    def write(parity, gradient):
        for z in range(4):
            for x in range(4):
                lanes = slice(128 * x, 128 * x + 128)
                old = cons[z * 4 + x, pl.ds(parity, 16, stride=2), :]
                turned[x, pl.ds(4 * parity + z, 16, stride=8), :] = (
                    old - gradient[16 * z : 16 * z + 16, lanes]
                )

    @pl.when(core[0] == 0)
    def _():
        write(0, near)
        write(1, far)

    @pl.when(core[0] == 1)
    def _():
        write(1, near)
        write(0, far)

    for x in range(4):
        out[:, 128 * x : 128 * x + 128] = turned[x]


def shards(volume, lift_weights, lift_bias, mix_weights, out_weights, projector, measured):
    core = lax.axis_index("c").reshape(1)
    pair = lax.ppermute(projector, "c", SWAP)

    packed = call(pack_kernel, shaped((32, 24, 128), F32), specs=[VM], nbytes=1 << 20)(volume[0])
    frames = lax.all_to_all(packed, ("q", "c"), split_axis=0, concat_axis=0, tiled=True)

    bias = jnp.broadcast_to(lift_bias[:, :, None], (3, 64, 3))
    lift = jnp.concatenate(
        [lift_weights.astype(F32), bias, jnp.zeros((3, 64, 2), F32)], axis=2
    )
    outw = jnp.broadcast_to(out_weights[:, :, None], (3, 64, 128))
    a1, a2, a3 = call(
        weights_kernel,
        (shaped((3, 512, 256), BF16), shaped((3, 256, 256), BF16), shaped((3, 256, 128), F32)),
        specs=[VM] * 3,
        flops=10**8,
        nbytes=1 << 20,
    )(lift, mix_weights, outw)

    vol, first, last = call(
        turn_kernel,
        (shaped((24, 48, 128), F32), shaped((6, 32, 128), BF16), shaped((6, 32, 128), BF16)),
        specs=[VM],
        nbytes=1 << 20,
    )(frames.reshape(768, 128))
    up = [(i, i + 1) for i in range(7)]
    before = lax.ppermute(last, "space", up)
    after = lax.ppermute(first, "space", [(j, i) for i, j in up])

    spread = pltpu.VMEM((3, 36, 48, 128), F32)
    xy = call(
        xy_kernel, shaped((16, 32, 128), F32), [spread], [VM] * 4, flops=12 * 10**9, nbytes=1 << 20
    )(vol, a1, a2, a3)
    cons, mine, other = call(
        rest_kernel,
        (shaped((16, 32, 128), F32), shaped((64, 512), BF16), shaped((64, 512), BF16)),
        [spread],
        [SM] + [VM] * 7,
        flops=24 * 10**9,
        nbytes=1 << 20,
    )(core, vol, before, after, xy, a1, a2, a3)

    theirs = lax.ppermute(other, "c", SWAP)
    partial = call(
        project_kernel,
        shaped((16, 8, 1024), BF16),
        [pltpu.VMEM((8, 128, 128), F32)],
        [VM] * 4,
        flops=3 * 10**8,
        nbytes=5 << 20,
    )(mine, theirs, projector, pair)
    parts = lax.all_to_all(partial, "q", split_axis=0, concat_axis=0, tiled=True)
    misfit = call(misfit_kernel, shaped((16, 8, 1024), BF16), specs=[VM] * 2)(
        parts, measured.reshape(8, 1024)
    )
    misfit = lax.all_to_all(misfit, "q", split_axis=0, concat_axis=0, tiled=True)
    near, far = call(
        gradient_kernel,
        (shaped((64, 512), F32), shaped((64, 512), F32)),
        [pltpu.VMEM((8, 128, 128), F32), pltpu.VMEM((64, 2048), BF16)],
        [VM] * 3,
        flops=3 * 10**8,
        nbytes=5 << 20,
    )(misfit, projector, pair)
    far = lax.ppermute(far, "c", SWAP)
    updated = call(
        update_kernel,
        shaped((128, 512), F32),
        [pltpu.VMEM((4, 128, 128), F32)],
        [SM] + [VM] * 3,
    )(core, cons, near, far)
    return updated.reshape(32, 4, 512)


def solution(mesh):
    fine = Mesh(mesh.devices.reshape(8, 16, 2), ("space", "q", "c"))
    tm = ("q", "c")
    placed = (
        P(tm, "space", None, None),
        P(),
        P(),
        P(),
        P(),
        P(None, tm),
        P(tm, "space", None),
    )
    return jax.shard_map(
        shards, mesh=fine, in_specs=placed, out_specs=P(None, "space", tm), check_vma=False
    )
```

```python
import jax
import jax.numpy as jnp
from jax import lax
from jax.experimental import pallas as pl
from jax.experimental.pallas import tpu as pltpu
from jax.sharding import Mesh, PartitionSpec as P

F32, BF16 = jnp.float32, jnp.bfloat16
VM = pl.BlockSpec(memory_space=pltpu.VMEM)
SM = pl.BlockSpec(memory_space=pltpu.SMEM)
SWAP = [(0, 1), (1, 0)]


def call(kernel, outs, scratch=(), specs=None, flops=0, nbytes=0, vmem=24):
    return pl.pallas_call(
        kernel,
        out_shape=outs,
        in_specs=specs,
        out_specs=jax.tree.map(lambda _: VM, outs),
        scratch_shapes=list(scratch),
        compiler_params=pltpu.CompilerParams(vmem_limit_bytes=vmem << 20),
        cost_estimate=pl.CostEstimate(flops=flops, bytes_accessed=nbytes, transcendentals=0),
    )


def shaped(shape, dtype):
    return jax.ShapeDtypeStruct(shape, dtype)


def iota(shape, dim):
    return lax.broadcasted_iota(jnp.int32, shape, dim)


def weights_kernel(lift, mix, outw, a1, a2, a3):
    spread = (iota((256, 64), 0) >> 2 == iota((256, 64), 1)).astype(F32).astype(BF16)
    spread_t = (iota((64, 256), 1) >> 2 == iota((64, 256), 0)).astype(F32).astype(BF16)
    taps = (iota((32, 256), 1) >> 3 == iota((32, 256), 0)).astype(F32).astype(BF16)
    row, col = iota((256, 256), 0) & 3, iota((256, 256), 1)
    part = iota((64, 32), 1)
    for k in range(3):
        full = lift[k]
        high = full.astype(BF16).astype(F32)
        mid = (full - high).astype(BF16).astype(F32)
        low = full - high - mid
        split = jnp.where(part == 28, mid, jnp.where(part == 29, low, high)).astype(BF16)
        base = jnp.dot(spread, split, preferred_element_type=F32).astype(BF16)
        base = jnp.dot(base, taps, preferred_element_type=F32)
        for half in range(2):
            a1[k, half * 256 : half * 256 + 256] = jnp.where(
                row + 4 * half == (col & 7), base, 0.0
            ).astype(BF16)
        mixed = jnp.dot(spread, mix[k], preferred_element_type=F32).astype(BF16)
        mixed = jnp.dot(mixed, spread_t, preferred_element_type=F32)
        a2[k] = jnp.where(row == (col & 3), mixed, 0.0).astype(BF16)
        a3[k] = jnp.dot(spread, outw[k], preferred_element_type=F32)


def pack_kernel(vol, out):
    zero = jnp.zeros((1, 128), F32)
    for p in range(16):
        for z in range(4):
            lo, hi = max(8 * p - 1, 0), min(8 * p + 9, 128)
            at = z * 10 + lo - (8 * p - 1)
            out[p, at : at + hi - lo] = vol[z, lo:hi]
            if p == 0:
                out[p, z * 10 : z * 10 + 1] = zero
            if p == 15:
                out[p, z * 10 + 9 : z * 10 + 10] = zero


def turn_kernel(rows, vol, half):
    for r in range(40):
        x = rows[pl.ds(r, 16, stride=40), :]
        vol[r] = x
        half[r] = x.astype(BF16)


def edges_kernel(vol, other, first, last):
    for r in range(10):
        first[r] = vol[r].astype(BF16)
        last[r] = vol[r + 30].astype(BF16)
        first[r + 10] = other[r]
        last[r + 10] = other[r + 30]


def spread_y(s, pos, v):
    lane = iota(v.shape, 1)
    s[0, pos] = jnp.where(lane == 0, 0.0, pltpu.roll(v, 1, 1))
    s[1, pos] = v
    s[2, pos] = jnp.where(lane == 127, 0.0, pltpu.roll(v, 127, 1))


def fill(c, own, theirs, pos, mine, other):
    spread_y(own, pos, mine)
    other = other.astype(F32)
    early = jnp.concatenate([jnp.zeros((1, 128), F32), other, jnp.zeros((7, 128), F32)], axis=0)
    late = jnp.concatenate([other, jnp.zeros((8, 128), F32)], axis=0)
    spread_y(theirs, pos, jnp.where(c == 0, early, late))


OFFSETS = (
    [(dt, db, da - 1) for dt in range(3) for da in range(3) for db in range(3)],
    [(dt, da, 10 * (db - 1)) for dt in range(3) for da in range(3) for db in range(3)],
    [(dt, 1, 10 * (da - 1) + db - 1) for dt in range(3) for da in range(3) for db in range(3)],
)


def corrected(own, theirs, a1, a2, a3, which, weight, pos, block):
    rows = []
    for dt, dy, step in OFFSETS[which]:
        s = own if dt == 1 else theirs
        at = pl.ds(8 * block + (dt == 2), 8)
        rows.append(
            jnp.concatenate([s[dy, pos + step, at, :], s[dy, pos + step + 1, at, :]], axis=1)
        )
    rows.append(jnp.ones((24, 256), F32))
    rows.append(jnp.zeros((16, 256), F32))
    taps = jnp.concatenate(rows, axis=0).astype(BF16)
    first = jnp.dot(a1[weight], taps, preferred_element_type=F32)
    first = jnp.maximum(first, 0.0).astype(BF16)
    w = a3[weight]
    w = jnp.concatenate([w, w], axis=1)
    sums = []
    for half in range(2):
        second = jnp.dot(
            a2[weight], first[half * 256 : half * 256 + 256], preferred_element_type=F32
        )
        second = jnp.maximum(second, 0.0) * w
        total = jnp.sum(second.reshape(32, 8, 256), axis=0)
        sums.append(total + pltpu.roll(total, 4, 0))
    return jnp.where(iota((8, 256), 0) < 4, sums[0], sums[1])


def xy_kernel(core, vol, other, a1, a2, a3, out, own, theirs):
    def load(r, carry):
        fill(core[0], own, theirs, r + 10, vol[r], other[r])
        return carry

    lax.fori_loop(0, 40, load, 0)

    def step(i, carry):
        z, x = i // 4, 2 * (i % 4)
        pos = (z + 1) * 10 + 1 + x
        for block in range(2):
            got = corrected(own, theirs, a1, a2, a3, 0, 0, pos, block)
            for j in range(2):
                out[z * 8 + x + j, 8 * block : 8 * block + 8] = got[:, 128 * j : 128 * j + 128]
        return carry

    lax.fori_loop(0, 16, step, 0)


def rest_kernel(core, vol, other, before, after, xy, a1, a2, a3, cons, image, own, theirs):
    def load(r, carry):
        fill(core[0], own, theirs, r + 10, vol[r], other[r])
        return carry

    lax.fori_loop(0, 40, load, 0)

    def load_edge(r, carry):
        fill(core[0], own, theirs, r, before[r].astype(F32), before[r + 10])
        fill(core[0], own, theirs, r + 50, after[r].astype(F32), after[r + 10])
        return carry

    lax.fori_loop(0, 10, load_edge, 0)

    def step(i, carry):
        z, x = i // 4, 2 * (i % 4)
        pos = (z + 1) * 10 + 1 + x
        for block in range(2):
            at = slice(8 * block, 8 * block + 8)
            got = corrected(own, theirs, a1, a2, a3, 1, 1, pos, block)
            got = got + corrected(own, theirs, a1, a2, a3, 2, 2, pos, block)
            for j in range(2):
                total = xy[z * 8 + x + j, at] + got[:, 128 * j : 128 * j + 128]
                cons[z * 8 + x + j, at] = vol[pos - 10 + j, at] + total / 3.0
        return carry

    lax.fori_loop(0, 16, step, 0)
    for z in range(4):
        for x in range(8):
            image[16 * z : 16 * z + 16, 128 * x : 128 * x + 128] = cons[z * 8 + x].astype(BF16)


def transpose_kernel(core, own, pair, out):
    c = core[0]

    def step(j, carry):
        rays = pl.ds(pl.multiple_of(256 * j, 256), 256)
        out[c, :, rays] = own[rays, :].T
        out[1 - c, :, rays] = pair[rays, :].T
        return carry

    lax.fori_loop(0, 8, step, 0)


def project_kernel(image, pixels, out, turned):
    for j in range(8):
        rays = slice(256 * j, 256 * j + 256)
        got = jnp.dot(image[:, :512], pixels[0, :, rays], preferred_element_type=F32)
        got = got + jnp.dot(image[:, 512:], pixels[1, :, rays], preferred_element_type=F32)
        for z in range(4):
            for n in range(2):
                turned[2 * (j % 4) + n, pl.ds(z * 2 + j // 4, 16, stride=8), :] = got[
                    16 * z : 16 * z + 16, 128 * n : 128 * n + 128
                ]
    for n in range(8):
        lanes = slice(128 * n, 128 * n + 128)
        for t in range(16):
            out[t, :, lanes] = turned[n, 8 * t : 8 * t + 8].astype(BF16)


def misfit_kernel(parts, measured, out):
    total = parts[0].astype(F32)
    for t in range(1, 16):
        total = total + parts[t].astype(F32)
    misfit = (total - measured[...]).astype(BF16)
    for t in range(16):
        out[t] = misfit


def far_kernel(core, misfit, pair, cons, far, rows, turned):
    for n in range(8):
        for t in range(16):
            turned[n, 8 * t : 8 * t + 8] = misfit[t, :, 128 * n : 128 * n + 128].astype(F32)
    for z in range(4):
        for half in range(2):
            for n in range(8):
                rows[16 * z : 16 * z + 16, 1024 * half + 128 * n : 1024 * half + 128 * n + 128] = (
                    turned[n, pl.ds(z * 2 + half, 16, stride=8), :].astype(BF16)
                )
    got = jnp.dot(rows[...], pair[...], preferred_element_type=F32)
    stepped(1 - core[0], cons, got, far)


def stepped(c, cons, gradient, out):
    for z in range(4):
        for x in range(4):
            at = (slice(16 * z, 16 * z + 16), slice(128 * x, 128 * x + 128))
            out[at] = cons[z * 8 + x + 4 * c] - gradient[at]


def near_kernel(core, rows, own, cons, near):
    got = jnp.dot(rows[...], own[...], preferred_element_type=F32)
    stepped(core[0], cons, got, near)


def merge_kernel(core, near, far, out, turned):
    def write(parity, rows):
        for z in range(4):
            for x in range(4):
                turned[x, pl.ds(4 * parity + z, 16, stride=8), :] = rows[
                    16 * z : 16 * z + 16, 128 * x : 128 * x + 128
                ]

    @pl.when(core[0] == 0)
    def _():
        write(0, near)
        write(1, far)

    @pl.when(core[0] == 1)
    def _():
        write(1, near)
        write(0, far)

    for x in range(4):
        for t in range(32):
            out[t, :, 128 * x : 128 * x + 128] = turned[x, 4 * t : 4 * t + 4]


def shards(volume, lift_weights, lift_bias, mix_weights, out_weights, projector, measured):
    core = lax.axis_index("c").reshape(1)
    packed = call(pack_kernel, shaped((16, 40, 128), F32), specs=[VM], nbytes=1 << 20)(volume[0])
    frames = lax.all_to_all(packed, "q", split_axis=0, concat_axis=0, tiled=True)

    pair = lax.ppermute(projector, "c", SWAP)
    bias = jnp.broadcast_to(lift_bias[:, :, None], (3, 64, 3))
    lift = jnp.concatenate(
        [lift_weights.astype(F32), bias, jnp.zeros((3, 64, 2), F32)], axis=2
    )
    outw = jnp.broadcast_to(out_weights[:, :, None], (3, 64, 128))
    a1, a2, a3 = call(
        weights_kernel,
        (shaped((3, 512, 256), BF16), shaped((3, 256, 256), BF16), shaped((3, 256, 128), F32)),
        specs=[VM] * 3,
        flops=10**8,
        nbytes=1 << 20,
    )(lift, mix_weights, outw)
    pixels = call(
        transpose_kernel,
        shaped((2, 512, 2048), BF16),
        specs=[SM, VM, VM],
        nbytes=8 << 20,
    )(core, projector, pair)

    vol, half = call(
        turn_kernel,
        (shaped((40, 16, 128), F32), shaped((40, 16, 128), BF16)),
        specs=[VM],
        nbytes=1 << 20,
    )(frames.reshape(640, 128))
    other = lax.ppermute(half, "c", SWAP)
    plane = shaped((20, 16, 128), BF16)
    first, last = call(edges_kernel, (plane, plane), specs=[VM] * 2)(vol, other)
    up = [(i, i + 1) for i in range(7)]
    before = lax.ppermute(last, "space", up)
    after = lax.ppermute(first, "space", [(j, i) for i, j in up])

    spread = [pltpu.VMEM((3, 60, 16, 128), F32), pltpu.VMEM((3, 60, 24, 128), F32)]
    xy = call(
        xy_kernel, shaped((32, 16, 128), F32), spread, [SM] + [VM] * 5, flops=12 * 10**9, nbytes=1 << 20
    )(core, vol, other, a1, a2, a3)
    cons, image = call(
        rest_kernel,
        (shaped((32, 16, 128), F32), shaped((64, 1024), BF16)),
        spread,
        [SM] + [VM] * 8,
        flops=24 * 10**9,
        nbytes=1 << 20,
    )(core, vol, other, before, after, xy, a1, a2, a3)

    partial = call(
        project_kernel,
        shaped((16, 8, 1024), BF16),
        [pltpu.VMEM((8, 128, 128), F32)],
        [VM] * 2,
        flops=3 * 10**8,
        nbytes=5 << 20,
    )(image, pixels)
    parts = lax.all_to_all(partial, "q", split_axis=0, concat_axis=0, tiled=True)
    misfit = call(misfit_kernel, shaped((16, 8, 1024), BF16), specs=[VM] * 2)(
        parts, measured.reshape(8, 1024)
    )
    misfit = lax.all_to_all(misfit, "q", split_axis=0, concat_axis=0, tiled=True)
    far, rows = call(
        far_kernel,
        (shaped((64, 512), F32), shaped((64, 2048), BF16)),
        [pltpu.VMEM((8, 128, 128), F32)],
        [SM] + [VM] * 3,
        flops=15 * 10**7,
        nbytes=3 << 20,
    )(core, misfit, pair, cons)
    far = lax.ppermute(far, "c", SWAP)
    near = call(
        near_kernel,
        shaped((64, 512), F32),
        specs=[SM] + [VM] * 3,
        flops=15 * 10**7,
        nbytes=3 << 20,
    )(core, rows, projector, cons)
    return call(
        merge_kernel,
        shaped((32, 4, 512), F32),
        [pltpu.VMEM((4, 128, 128), F32)],
        [SM] + [VM] * 2,
    )(core, near, far)


def solution(mesh):
    fine = Mesh(mesh.devices.reshape(8, 16, 2), ("space", "q", "c"))
    tm = ("q", "c")
    placed = (
        P(tm, "space", None, None),
        P(),
        P(),
        P(),
        P(),
        P(None, tm),
        P(tm, "space", None),
    )
    return jax.shard_map(
        shards, mesh=fine, in_specs=placed, out_specs=P(None, "space", tm), check_vma=False
    )
```

```python
import jax
import jax.numpy as jnp
from jax import lax
from jax.experimental import pallas as pl
from jax.experimental.pallas import tpu as pltpu
from jax.sharding import Mesh, PartitionSpec as P

F32, BF16 = jnp.float32, jnp.bfloat16
VM = pl.BlockSpec(memory_space=pltpu.VMEM)
SM = pl.BlockSpec(memory_space=pltpu.SMEM)
SWAP = [(0, 1), (1, 0)]


def call(kernel, outs, scratch=(), specs=None, flops=0, nbytes=0, vmem=24, aliases=None):
    return pl.pallas_call(
        kernel,
        out_shape=outs,
        in_specs=specs,
        out_specs=jax.tree.map(lambda _: VM, outs),
        scratch_shapes=list(scratch),
        input_output_aliases=aliases or {},
        compiler_params=pltpu.CompilerParams(vmem_limit_bytes=vmem << 20),
        cost_estimate=pl.CostEstimate(flops=flops, bytes_accessed=nbytes, transcendentals=0),
    )


def shaped(shape, dtype):
    return jax.ShapeDtypeStruct(shape, dtype)


def iota(shape, dim):
    return lax.broadcasted_iota(jnp.int32, shape, dim)


def weights_kernel(lift, mix, outw, a1, a2, a3):
    spread = (iota((256, 64), 0) >> 2 == iota((256, 64), 1)).astype(F32).astype(BF16)
    spread_t = (iota((64, 256), 1) >> 2 == iota((64, 256), 0)).astype(F32).astype(BF16)
    taps = (iota((32, 256), 1) >> 3 == iota((32, 256), 0)).astype(F32).astype(BF16)
    row, col = iota((256, 256), 0) & 3, iota((256, 256), 1)
    part = iota((64, 32), 1)
    for k in range(3):
        full = lift[k]
        high = full.astype(BF16).astype(F32)
        mid = (full - high).astype(BF16).astype(F32)
        low = full - high - mid
        split = jnp.where(part == 28, mid, jnp.where(part == 29, low, high)).astype(BF16)
        base = jnp.dot(spread, split, preferred_element_type=F32).astype(BF16)
        base = jnp.dot(base, taps, preferred_element_type=F32)
        for half in range(2):
            a1[k, half * 256 : half * 256 + 256] = jnp.where(
                row + 4 * half == (col & 7), base, 0.0
            ).astype(BF16)
        mixed = jnp.dot(spread, mix[k], preferred_element_type=F32).astype(BF16)
        mixed = jnp.dot(mixed, spread_t, preferred_element_type=F32)
        a2[k] = jnp.where(row == (col & 3), mixed, 0.0).astype(BF16)
        a3[k] = jnp.dot(spread, outw[k], preferred_element_type=F32)


def pack_kernel(vol, out):
    zero = jnp.zeros((1, 128), F32)
    for p in range(16):
        for z in range(4):
            lo, hi = max(8 * p - 1, 0), min(8 * p + 9, 128)
            at = z * 10 + lo - (8 * p - 1)
            out[p, at : at + hi - lo] = vol[z, lo:hi]
            if p == 0:
                out[p, z * 10 : z * 10 + 1] = zero
            if p == 15:
                out[p, z * 10 + 9 : z * 10 + 10] = zero


def turn_kernel(rows, vol, half):
    for r in range(40):
        x = rows[pl.ds(r, 16, stride=40), :]
        vol[r] = x
        half[r] = x.astype(BF16)


def spread_y(s, pos, at, v):
    lane = iota((8, 128), 1)
    s[0, pos, at] = jnp.where(lane == 0, 0.0, pltpu.roll(v, 1, 1))
    s[1, pos, at] = v
    s[2, pos, at] = jnp.where(lane == 127, 0.0, pltpu.roll(v, 127, 1))


def spread_frames(core, padded, places, own, theirs, mine, other):
    zero = jnp.zeros((8, 128), F32)
    for r, pos in enumerate(places):
        padded[r, 0:8] = zero
        padded[r, 8:24] = other(r).astype(F32)
        padded[r, 24:32] = zero
        for j in range(2):
            spread_y(own, pos, slice(8 * j, 8 * j + 8), mine(r)[8 * j : 8 * j + 8].astype(F32))

    def write(start):
        for r, pos in enumerate(places):
            for j in range(3):
                got = padded[r, pl.ds(start + 8 * j, 8), :]
                spread_y(theirs, pos, slice(8 * j, 8 * j + 8), got)

    @pl.when(core[0] == 0)
    def _():
        write(7)

    @pl.when(core[0] == 1)
    def _():
        write(8)


def spread_kernel(core, vol, other, own, theirs, first, last, padded):
    for r in range(10):
        first[r] = vol[r].astype(BF16)
        last[r] = vol[r + 30].astype(BF16)
        first[r + 10] = other[r]
        last[r + 10] = other[r + 30]
    spread_frames(
        core, padded, range(10, 50), own, theirs, lambda r: vol[r], lambda r: other[r]
    )


OFFSETS = (
    [(dt, db, da - 1) for dt in range(3) for da in range(3) for db in range(3)],
    [(dt, da, 10 * (db - 1)) for dt in range(3) for da in range(3) for db in range(3)],
    [(dt, 1, 10 * (da - 1) + db - 1) for dt in range(3) for da in range(3) for db in range(3)],
)


def corrected(own, theirs, a1, a2, a3, which, weight, pos, block):
    rows = []
    for dt, dy, step in OFFSETS[which]:
        s = own if dt == 1 else theirs
        at = pl.ds(8 * block + (dt == 2), 8)
        rows.append(
            jnp.concatenate([s[dy, pos + step, at, :], s[dy, pos + step + 1, at, :]], axis=1)
        )
    rows.append(jnp.ones((24, 256), F32))
    rows.append(jnp.zeros((16, 256), F32))
    taps = jnp.concatenate(rows, axis=0).astype(BF16)
    first = jnp.dot(a1[weight], taps, preferred_element_type=F32)
    first = jnp.maximum(first, 0.0).astype(BF16)
    w = a3[weight]
    w = jnp.concatenate([w, w], axis=1)
    sums = []
    for half in range(2):
        second = jnp.dot(
            a2[weight], first[half * 256 : half * 256 + 256], preferred_element_type=F32
        )
        second = jnp.maximum(second, 0.0) * w
        total = jnp.sum(second.reshape(32, 8, 256), axis=0)
        sums.append(total + pltpu.roll(total, 4, 0))
    return jnp.where(iota((8, 256), 0) < 4, sums[0], sums[1])


def xy_kernel(own, theirs, a1, a2, a3, out):
    def step(i, carry):
        z, x = i // 4, 2 * (i % 4)
        pos = (z + 1) * 10 + 1 + x
        for block in range(2):
            got = corrected(own, theirs, a1, a2, a3, 0, 0, pos, block)
            for j in range(2):
                out[z * 8 + x + j, 8 * block : 8 * block + 8] = got[:, 128 * j : 128 * j + 128]
        return carry

    lax.fori_loop(0, 16, step, 0)


def rest_kernel(
    core, vol, before, after, xy, a1, a2, a3, own_in, theirs_in, cons, image, own, theirs, padded
):
    def pick(offset):
        return lambda r: before[r + offset] if r < 10 else after[r - 10 + offset]

    places = list(range(10)) + list(range(50, 60))
    spread_frames(core, padded, places, own, theirs, pick(0), pick(10))

    def step(i, carry):
        z, x = i // 4, 2 * (i % 4)
        pos = (z + 1) * 10 + 1 + x
        for block in range(2):
            at = slice(8 * block, 8 * block + 8)
            got = corrected(own, theirs, a1, a2, a3, 1, 1, pos, block)
            got = got + corrected(own, theirs, a1, a2, a3, 2, 2, pos, block)
            for j in range(2):
                total = xy[z * 8 + x + j, at] + got[:, 128 * j : 128 * j + 128]
                cons[z * 8 + x + j, at] = vol[pos - 10 + j, at] + total / 3.0
        return carry

    lax.fori_loop(0, 16, step, 0)
    for z in range(4):
        for x in range(8):
            image[16 * z : 16 * z + 16, 128 * x : 128 * x + 128] = cons[z * 8 + x].astype(BF16)


def transpose_kernel(core, own, pair, out):
    c = core[0]

    def step(j, carry):
        rays = pl.ds(pl.multiple_of(256 * j, 256), 256)
        out[c, :, rays] = own[rays, :].T
        out[1 - c, :, rays] = pair[rays, :].T
        return carry

    lax.fori_loop(0, 8, step, 0)


def project_kernel(image, pixels, out, turned):
    for j in range(8):
        rays = slice(256 * j, 256 * j + 256)
        got = jnp.dot(image[:, :512], pixels[0, :, rays], preferred_element_type=F32)
        got = got + jnp.dot(image[:, 512:], pixels[1, :, rays], preferred_element_type=F32)
        for z in range(4):
            for n in range(2):
                turned[2 * (j % 4) + n, pl.ds(z * 2 + j // 4, 16, stride=8), :] = got[
                    16 * z : 16 * z + 16, 128 * n : 128 * n + 128
                ]
    for n in range(8):
        lanes = slice(128 * n, 128 * n + 128)
        for t in range(16):
            out[t, :, lanes] = turned[n, 8 * t : 8 * t + 8].astype(BF16)


def misfit_kernel(parts, measured, out):
    total = parts[0].astype(F32)
    for t in range(1, 16):
        total = total + parts[t].astype(F32)
    misfit = (total - measured[...]).astype(BF16)
    for t in range(16):
        out[t] = misfit


def far_kernel(core, misfit, pair, cons, far, rows, turned):
    for n in range(8):
        for t in range(16):
            turned[n, 8 * t : 8 * t + 8] = misfit[t, :, 128 * n : 128 * n + 128].astype(F32)
    for z in range(4):
        for half in range(2):
            for n in range(8):
                rows[16 * z : 16 * z + 16, 1024 * half + 128 * n : 1024 * half + 128 * n + 128] = (
                    turned[n, pl.ds(z * 2 + half, 16, stride=8), :].astype(BF16)
                )
    got = jnp.dot(rows[...], pair[...], preferred_element_type=F32)
    stepped(1 - core[0], cons, got, far)


def stepped(c, cons, gradient, out):
    for z in range(4):
        for x in range(4):
            at = (slice(16 * z, 16 * z + 16), slice(128 * x, 128 * x + 128))
            out[at] = cons[z * 8 + x + 4 * c] - gradient[at]


def near_kernel(core, rows, own, cons, near):
    got = jnp.dot(rows[...], own[...], preferred_element_type=F32)
    stepped(core[0], cons, got, near)


def merge_kernel(core, near, far, out, turned):
    def write(parity, rows):
        for z in range(4):
            for x in range(4):
                turned[x, pl.ds(4 * parity + z, 16, stride=8), :] = rows[
                    16 * z : 16 * z + 16, 128 * x : 128 * x + 128
                ]

    @pl.when(core[0] == 0)
    def _():
        write(0, near)
        write(1, far)

    @pl.when(core[0] == 1)
    def _():
        write(1, near)
        write(0, far)

    for x in range(4):
        for t in range(32):
            out[t, :, 128 * x : 128 * x + 128] = turned[x, 4 * t : 4 * t + 4]


def shards(volume, lift_weights, lift_bias, mix_weights, out_weights, projector, measured):
    core = lax.axis_index("c").reshape(1)
    packed = call(pack_kernel, shaped((16, 40, 128), F32), specs=[VM], nbytes=1 << 20)(volume[0])
    frames = lax.all_to_all(packed, "q", split_axis=0, concat_axis=0, tiled=True)

    pair = lax.ppermute(projector, "c", SWAP)
    bias = jnp.broadcast_to(lift_bias[:, :, None], (3, 64, 3))
    lift = jnp.concatenate(
        [lift_weights.astype(F32), bias, jnp.zeros((3, 64, 2), F32)], axis=2
    )
    outw = jnp.broadcast_to(out_weights[:, :, None], (3, 64, 128))
    a1, a2, a3 = call(
        weights_kernel,
        (shaped((3, 512, 256), BF16), shaped((3, 256, 256), BF16), shaped((3, 256, 128), F32)),
        specs=[VM] * 3,
        flops=10**8,
        nbytes=1 << 20,
    )(lift, mix_weights, outw)
    pixels = call(
        transpose_kernel,
        shaped((2, 512, 2048), BF16),
        specs=[SM, VM, VM],
        nbytes=8 << 20,
    )(core, projector, pair)
    frames, a1, a2, a3, pixels = lax.optimization_barrier((frames, a1, a2, a3, pixels))

    vol, half = call(
        turn_kernel,
        (shaped((40, 16, 128), F32), shaped((40, 16, 128), BF16)),
        specs=[VM],
        nbytes=1 << 20,
    )(frames.reshape(640, 128))
    other = lax.ppermute(half, "c", SWAP)
    plane = shaped((20, 16, 128), BF16)
    own, theirs = shaped((3, 60, 16, 128), F32), shaped((3, 60, 24, 128), F32)
    own, theirs, first, last = call(
        spread_kernel,
        (own, theirs, plane, plane),
        [pltpu.VMEM((40, 32, 128), F32)],
        [SM, VM, VM],
        nbytes=8 << 20,
    )(core, vol, other)
    up = [(i, i + 1) for i in range(7)]
    before = lax.ppermute(last, "space", up)
    after = lax.ppermute(first, "space", [(j, i) for i, j in up])

    xy = call(
        xy_kernel, shaped((32, 16, 128), F32), (), [VM] * 5, flops=12 * 10**9, nbytes=1 << 20
    )(own, theirs, a1, a2, a3)
    cons, image, _, _ = call(
        rest_kernel,
        (
            shaped((32, 16, 128), F32),
            shaped((64, 1024), BF16),
            shaped((3, 60, 16, 128), F32),
            shaped((3, 60, 24, 128), F32),
        ),
        [pltpu.VMEM((20, 32, 128), F32)],
        [SM] + [VM] * 9,
        flops=24 * 10**9,
        nbytes=1 << 20,
        aliases={8: 2, 9: 3},
    )(core, vol, before, after, xy, a1, a2, a3, own, theirs)

    partial = call(
        project_kernel,
        shaped((16, 8, 1024), BF16),
        [pltpu.VMEM((8, 128, 128), F32)],
        [VM] * 2,
        flops=3 * 10**8,
        nbytes=5 << 20,
    )(image, pixels)
    parts = lax.all_to_all(partial, "q", split_axis=0, concat_axis=0, tiled=True)
    misfit = call(misfit_kernel, shaped((16, 8, 1024), BF16), specs=[VM] * 2)(
        parts, measured.reshape(8, 1024)
    )
    misfit = lax.all_to_all(misfit, "q", split_axis=0, concat_axis=0, tiled=True)
    far, rows = call(
        far_kernel,
        (shaped((64, 512), F32), shaped((64, 2048), BF16)),
        [pltpu.VMEM((8, 128, 128), F32)],
        [SM] + [VM] * 3,
        flops=15 * 10**7,
        nbytes=3 << 20,
    )(core, misfit, pair, cons)
    far = lax.ppermute(far, "c", SWAP)
    near = call(
        near_kernel,
        shaped((64, 512), F32),
        specs=[SM] + [VM] * 3,
        flops=15 * 10**7,
        nbytes=3 << 20,
    )(core, rows, projector, cons)
    return call(
        merge_kernel,
        shaped((32, 4, 512), F32),
        [pltpu.VMEM((4, 128, 128), F32)],
        [SM] + [VM] * 2,
    )(core, near, far)


def solution(mesh):
    fine = Mesh(mesh.devices.reshape(8, 16, 2), ("space", "q", "c"))
    tm = ("q", "c")
    placed = (
        P(tm, "space", None, None),
        P(),
        P(),
        P(),
        P(),
        P(None, tm),
        P(tm, "space", None),
    )
    return jax.shard_map(
        shards, mesh=fine, in_specs=placed, out_specs=P(None, "space", tm), check_vma=False
    )
```

```python
import jax
import jax.numpy as jnp
from jax import lax
from jax.experimental import pallas as pl
from jax.experimental.pallas import tpu as pltpu
from jax.sharding import Mesh, PartitionSpec as P

F32, BF16 = jnp.float32, jnp.bfloat16
VM = pl.BlockSpec(memory_space=pltpu.VMEM)
SM = pl.BlockSpec(memory_space=pltpu.SMEM)
SWAP = [(0, 1), (1, 0)]


def call(kernel, outs, scratch=(), specs=None, flops=0, nbytes=0, vmem=24, aliases=None):
    return pl.pallas_call(
        kernel,
        out_shape=outs,
        in_specs=specs,
        out_specs=jax.tree.map(lambda _: VM, outs),
        scratch_shapes=list(scratch),
        input_output_aliases=aliases or {},
        compiler_params=pltpu.CompilerParams(vmem_limit_bytes=vmem << 20),
        cost_estimate=pl.CostEstimate(flops=flops, bytes_accessed=nbytes, transcendentals=0),
    )


def shaped(shape, dtype):
    return jax.ShapeDtypeStruct(shape, dtype)


def iota(shape, dim):
    return lax.broadcasted_iota(jnp.int32, shape, dim)


def weights_kernel(lift, bias, mix, outw, a1, a2, a3):
    spread = (iota((256, 64), 0) >> 2 == iota((256, 64), 1)).astype(F32)
    spread_t = (iota((64, 256), 1) >> 2 == iota((64, 256), 0)).astype(F32).astype(BF16)
    taps = (iota((27, 256), 1) >> 3 == iota((27, 256), 0)).astype(F32).astype(BF16)
    row, col = iota((256, 256), 0) & 3, iota((256, 256), 1)
    tap = col >> 3

    def column(values):
        return jnp.sum(spread * values, axis=1, keepdims=True)

    for k in range(3):
        full = bias[k : k + 1, :]
        high = full.astype(BF16).astype(F32)
        mid = (full - high).astype(BF16).astype(F32)
        low = full - high - mid
        base = jnp.dot(spread.astype(BF16), lift[k], preferred_element_type=F32).astype(BF16)
        base = jnp.dot(base, taps, preferred_element_type=F32)
        for at, part in ((27, high), (28, mid), (29, low)):
            base = jnp.where(tap == at, column(part), base)
        for half in range(2):
            a1[k, half * 256 : half * 256 + 256] = jnp.where(
                row + 4 * half == (col & 7), base, 0.0
            ).astype(BF16)
        mixed = jnp.dot(spread.astype(BF16), mix[k], preferred_element_type=F32).astype(BF16)
        mixed = jnp.dot(mixed, spread_t, preferred_element_type=F32)
        a2[k] = jnp.where(row == (col & 3), mixed, 0.0).astype(BF16)
        a3[k] = jnp.broadcast_to(column(outw[...].astype(F32)[k : k + 1, :]), (256, 128))


def spread_plane(s, t, z, plane):
    zero = jnp.zeros((8, 128), F32)
    lane = iota((8, 128), 1)
    for dy in range(3):
        s[t, z, dy, 0:8] = zero
        s[t, z, dy, 136:144] = zero
    for j in range(8):
        pair = plane[16 * j : 16 * j + 16].astype(F32)
        for i in range(2):
            v = pair[8 * i : 8 * i + 8]
            at = slice(16 * j + 8 * i + 8, 16 * j + 8 * i + 16)
            s[t, z, 0, at] = jnp.where(lane == 0, 0.0, pltpu.roll(v, 1, 1))
            s[t, z, 1, at] = v
            s[t, z, 2, at] = jnp.where(lane == 127, 0.0, pltpu.roll(v, 127, 1))


def spread_kernel(core, mine, near, next_, s, first, last):
    c = core[0]
    for i, ref in enumerate((mine, near, next_)):
        first[i] = ref[0]
        last[i] = ref[3]

    def step(z, carry):
        spread_plane(s, 1, z + 1, mine[z])
        spread_plane(s, 2 - 2 * c, z + 1, near[z])
        spread_plane(s, 2 * c, z + 1, next_[z])
        return carry

    lax.fori_loop(0, 4, step, 0)


OFFSETS = (
    [(dt, 1, db, da) for dt in range(3) for da in range(3) for db in range(3)],
    [(dt, db, da, 1) for dt in range(3) for da in range(3) for db in range(3)],
    [(dt, da, 1, db) for dt in range(3) for da in range(3) for db in range(3)],
)


def corrected(s, a1, a2, a3, which, z, block):
    rows = []
    for dt, dz, dy, dx in OFFSETS[which]:
        at = 7 + dx + 16 * block
        rows.append(
            jnp.concatenate(
                [s[dt, z + dz, dy, at : at + 8], s[dt, z + dz, dy, at + 8 : at + 16]], axis=1
            )
        )
    rows.append(jnp.ones((24, 256), F32))
    rows.append(jnp.zeros((16, 256), F32))
    taps = jnp.concatenate(rows, axis=0).astype(BF16)
    first = jnp.dot(a1[which], taps, preferred_element_type=F32)
    first = jnp.maximum(first, 0.0).astype(BF16)
    w = a3[which]
    w = jnp.concatenate([w, w], axis=1)
    sums = []
    for half in range(2):
        second = jnp.dot(
            a2[which], first[half * 256 : half * 256 + 256], preferred_element_type=F32
        )
        second = jnp.maximum(second, 0.0) * w
        total = jnp.sum(second.reshape(32, 8, 256), axis=0)
        sums.append(total + pltpu.roll(total, 4, 0))
    return jnp.where(iota((8, 256), 0) < 4, sums[0], sums[1])


def xy_kernel(s, a1, a2, a3, out):
    def step(i, carry):
        for z in (2 * i, 2 * i + 1):
            for block in range(8):
                got = corrected(s, a1, a2, a3, 0, z, block)
                out[2 * block, z] = got[:, :128]
                out[2 * block + 1, z] = got[:, 128:]
        return carry

    lax.fori_loop(0, 2, step, 0)


def rest_kernel(core, vol, before, after, xy, a1, a2, a3, s_in, cons, s):
    c = core[0]
    for i, t in enumerate((1, 2 - 2 * c, 2 * c)):
        spread_plane(s, t, 0, before[i])
        spread_plane(s, t, 5, after[i])

    def step(z, carry):
        for block in range(8):
            got = corrected(s, a1, a2, a3, 1, z, block)
            got = got + corrected(s, a1, a2, a3, 2, z, block)
            for j in range(2):
                at = 2 * block + j
                total = xy[at, z] + got[:, 128 * j : 128 * j + 128]
                cons[at, z] = vol[z, 8 * at : 8 * at + 8] + total / 3.0
        return carry

    lax.fori_loop(0, 4, step, 0)


def transpose_kernel(core, own, pair, out):
    c = core[0]

    def step(j, carry):
        rays = pl.ds(pl.multiple_of(256 * j, 256), 256)
        out[c, :, rays] = own[rays, :].T
        out[1 - c, :, rays] = pair[rays, :].T
        return carry

    lax.fori_loop(0, 8, step, 0)


def project_kernel(blocks, pixels, out, cons, image, turned):
    for z in range(4):
        for x in range(8):
            got = blocks[pl.ds(z * 8 + x, 16, stride=32), :]
            cons[z * 8 + x] = got
            image[16 * z : 16 * z + 16, 128 * x : 128 * x + 128] = got.astype(BF16)
    for j in range(8):
        rays = slice(256 * j, 256 * j + 256)
        got = jnp.dot(image[:, 0:512], pixels[0, :, rays], preferred_element_type=F32)
        got = got + jnp.dot(image[:, 512:1024], pixels[1, :, rays], preferred_element_type=F32)
        for z in range(4):
            for n in range(2):
                turned[2 * (j % 4) + n, pl.ds(z * 2 + j // 4, 16, stride=8), :] = got[
                    16 * z : 16 * z + 16, 128 * n : 128 * n + 128
                ]
    for n in range(8):
        lanes = slice(128 * n, 128 * n + 128)
        for t in range(16):
            out[t, :, lanes] = turned[n, 8 * t : 8 * t + 8].astype(BF16)


def misfit_kernel(parts, measured, out):
    total = parts[0].astype(F32)
    for t in range(1, 16):
        total = total + parts[t].astype(F32)
    misfit = (total - measured[...]).astype(BF16)
    for t in range(16):
        out[t] = misfit


def far_kernel(core, misfit, pair, cons, far, rows, turned):
    for n in range(8):
        for t in range(16):
            turned[n, 8 * t : 8 * t + 8] = misfit[t, :, 128 * n : 128 * n + 128].astype(F32)
    for z in range(4):
        for half in range(2):
            for n in range(8):
                rows[16 * z : 16 * z + 16, 1024 * half + 128 * n : 1024 * half + 128 * n + 128] = (
                    turned[n, pl.ds(z * 2 + half, 16, stride=8), :].astype(BF16)
                )
    got = jnp.dot(rows[...], pair[...], preferred_element_type=F32)
    stepped(1 - core[0], cons, got, far)


def stepped(c, cons, gradient, out):
    for z in range(4):
        for x in range(4):
            at = (slice(16 * z, 16 * z + 16), slice(128 * x, 128 * x + 128))
            out[at] = cons[z * 8 + x + 4 * c] - gradient[at]


def near_kernel(core, rows, own, cons, near):
    got = jnp.dot(rows[...], own[...], preferred_element_type=F32)
    stepped(core[0], cons, got, near)


def merge_kernel(core, near, far, out, turned):
    def write(parity, rows):
        for z in range(4):
            for x in range(4):
                turned[x, pl.ds(4 * parity + z, 16, stride=8), :] = rows[
                    16 * z : 16 * z + 16, 128 * x : 128 * x + 128
                ]

    @pl.when(core[0] == 0)
    def _():
        write(0, near)
        write(1, far)

    @pl.when(core[0] == 1)
    def _():
        write(1, near)
        write(0, far)

    for x in range(4):
        for t in range(32):
            out[t, :, 128 * x : 128 * x + 128] = turned[x, 4 * t : 4 * t + 4]


def shards(volume, lift_weights, lift_bias, mix_weights, out_weights, projector, measured):
    core = lax.axis_index("c").reshape(1)
    coarse = volume[0].astype(BF16)
    near = lax.ppermute(coarse, "c", SWAP)
    up = [(2 * i + 1, 2 * i + 2) for i in range(15)]
    next_ = lax.ppermute(coarse, ("q", "c"), up + [(j, i) for i, j in up])
    pair = lax.ppermute(projector, "c", SWAP)

    a1, a2, a3 = call(
        weights_kernel,
        (shaped((3, 512, 256), BF16), shaped((3, 256, 256), BF16), shaped((3, 256, 128), F32)),
        specs=[VM] * 4,
        flops=10**8,
        nbytes=1 << 20,
    )(lift_weights, lift_bias, mix_weights, out_weights)
    planes, plane = shaped((3, 6, 3, 144, 128), F32), shaped((3, 128, 128), BF16)
    s, first, last = call(
        spread_kernel, (planes, plane, plane), specs=[SM] + [VM] * 3, nbytes=8 << 20
    )(core, coarse, near, next_)
    up = [(i, i + 1) for i in range(7)]
    before = lax.ppermute(last, "space", up)
    after = lax.ppermute(first, "space", [(j, i) for i, j in up])

    blocks = shaped((16, 4, 8, 128), F32)
    xy = call(xy_kernel, blocks, specs=[VM] * 4, flops=12 * 10**9, nbytes=1 << 20)(s, a1, a2, a3)
    consensus, _ = call(
        rest_kernel,
        (blocks, planes),
        specs=[SM] + [VM] * 8,
        flops=24 * 10**9,
        nbytes=1 << 20,
        aliases={8: 1},
    )(core, volume[0], before, after, xy, a1, a2, a3, s)
    frames = lax.all_to_all(
        consensus.reshape(16, 32, 128), "q", split_axis=0, concat_axis=0, tiled=True
    )
    pixels = call(
        transpose_kernel,
        shaped((2, 512, 2048), BF16),
        specs=[SM, VM, VM],
        nbytes=8 << 20,
    )(core, projector, pair)

    partial, cons = call(
        project_kernel,
        (shaped((16, 8, 1024), BF16), shaped((32, 16, 128), F32)),
        [pltpu.VMEM((64, 1024), BF16), pltpu.VMEM((8, 128, 128), F32)],
        [VM] * 2,
        flops=3 * 10**8,
        nbytes=5 << 20,
    )(frames.reshape(512, 128), pixels)
    parts = lax.all_to_all(partial, "q", split_axis=0, concat_axis=0, tiled=True)
    misfit = call(misfit_kernel, shaped((16, 8, 1024), BF16), specs=[VM] * 2)(
        parts, measured.reshape(8, 1024)
    )
    misfit = lax.all_to_all(misfit, "q", split_axis=0, concat_axis=0, tiled=True)
    far, rows = call(
        far_kernel,
        (shaped((64, 512), F32), shaped((64, 2048), BF16)),
        [pltpu.VMEM((8, 128, 128), F32)],
        [SM] + [VM] * 3,
        flops=15 * 10**7,
        nbytes=3 << 20,
    )(core, misfit, pair, cons)
    far = lax.ppermute(far, "c", SWAP)
    near = call(
        near_kernel,
        shaped((64, 512), F32),
        specs=[SM] + [VM] * 3,
        flops=15 * 10**7,
        nbytes=3 << 20,
    )(core, rows, projector, cons)
    return call(
        merge_kernel,
        shaped((32, 4, 512), F32),
        [pltpu.VMEM((4, 128, 128), F32)],
        [SM] + [VM] * 2,
    )(core, near, far)


def solution(mesh):
    fine = Mesh(mesh.devices.reshape(8, 16, 2), ("space", "q", "c"))
    tm = ("q", "c")
    placed = (
        P(tm, "space", None, None),
        P(),
        P(),
        P(),
        P(),
        P(None, tm),
        P(tm, "space", None),
    )
    return jax.shard_map(
        shards, mesh=fine, in_specs=placed, out_specs=P(None, "space", tm), check_vma=False
    )
```

```python
import jax
import jax.numpy as jnp
from jax import lax
from jax.experimental import pallas as pl
from jax.experimental.pallas import tpu as pltpu
from jax.sharding import Mesh, PartitionSpec as P

F32, BF16 = jnp.float32, jnp.bfloat16
VM = pl.BlockSpec(memory_space=pltpu.VMEM)
SM = pl.BlockSpec(memory_space=pltpu.SMEM)
HB = pl.BlockSpec(memory_space=pltpu.HBM)
SWAP = [(0, 1), (1, 0)]
NT = (((1,), (1,)), ((), ()))


def call(kernel, outs, scratch=(), specs=None, flops=0, nbytes=0, vmem=24, aliases=None):
    return pl.pallas_call(
        kernel,
        out_shape=outs,
        in_specs=specs,
        out_specs=jax.tree.map(lambda _: VM, outs),
        scratch_shapes=list(scratch),
        input_output_aliases=aliases or {},
        compiler_params=pltpu.CompilerParams(vmem_limit_bytes=vmem << 20),
        cost_estimate=pl.CostEstimate(flops=flops, bytes_accessed=nbytes, transcendentals=0),
    )


def shaped(shape, dtype):
    return jax.ShapeDtypeStruct(shape, dtype)


def iota(shape, dim):
    return lax.broadcasted_iota(jnp.int32, shape, dim)


def weights_kernel(matrices, vectors, a1, a2, a3):
    spread = (iota((256, 64), 0) >> 2 == iota((256, 64), 1)).astype(F32)
    spread_t = (iota((64, 256), 1) >> 2 == iota((64, 256), 0)).astype(F32).astype(BF16)
    taps = (iota((27, 256), 1) >> 3 == iota((27, 256), 0)).astype(F32).astype(BF16)
    row, col = iota((256, 256), 0) & 3, iota((256, 256), 1)
    tap = col >> 3
    spread_b = spread.astype(BF16)

    def column(values):
        return jnp.sum(spread * values, axis=1, keepdims=True)

    for k in range(3):
        full = vectors[0, k : k + 1]
        high = full.astype(BF16).astype(F32)
        mid = (full - high).astype(BF16).astype(F32)
        low = full - high - mid
        base = lax.dot_general(spread_b, matrices[k, 64:91], NT, preferred_element_type=F32).astype(BF16)
        base = jnp.dot(base, taps, preferred_element_type=F32)
        for at, part in ((27, high), (28, mid), (29, low)):
            base = jnp.where(tap == at, column(part), base)
        for half in range(2):
            a1[k, half * 256 : half * 256 + 256] = jnp.where(
                row + 4 * half == (col & 7), base, 0.0
            ).astype(BF16)
        mixed = jnp.dot(spread_b, matrices[k, 0:64], preferred_element_type=F32).astype(BF16)
        mixed = jnp.dot(mixed, spread_t, preferred_element_type=F32)
        a2[k] = jnp.where(row == (col & 3), mixed, 0.0).astype(BF16)
        a3[k] = jnp.broadcast_to(column(vectors[1, k : k + 1]), (256, 128))


def spread_plane(s, t, z, plane):
    zero = jnp.zeros((8, 128), F32)
    lane = iota((8, 128), 1)
    for dy in range(3):
        s[t, z, dy, 0:8] = zero
        s[t, z, dy, 136:144] = zero
    for j in range(8):
        pair = plane[16 * j : 16 * j + 16].astype(F32)
        for i in range(2):
            v = pair[8 * i : 8 * i + 8]
            at = slice(16 * j + 8 * i + 8, 16 * j + 8 * i + 16)
            s[t, z, 0, at] = jnp.where(lane == 0, 0.0, pltpu.roll(v, 1, 1))
            s[t, z, 1, at] = v
            s[t, z, 2, at] = jnp.where(lane == 127, 0.0, pltpu.roll(v, 127, 1))


def spread_kernel(core, parity, mine, near, next_, s, to_near, to_next):
    c, odd = core[0], parity[0]
    for i, ref in enumerate((mine, near, next_)):
        to_near[i] = ref[3 - 3 * odd]
        to_next[i] = ref[3 * odd]

    def step(z, carry):
        spread_plane(s, 1, z + 1, mine[z])
        spread_plane(s, 2 - 2 * c, z + 1, near[z])
        spread_plane(s, 2 * c, z + 1, next_[z])
        return carry

    lax.fori_loop(0, 4, step, 0)


OFFSETS = (
    [(dt, 1, db, da) for dt in range(3) for da in range(3) for db in range(3)],
    [(dt, db, da, 1) for dt in range(3) for da in range(3) for db in range(3)],
    [(dt, da, 1, db) for dt in range(3) for da in range(3) for db in range(3)],
)


def corrected(s, a1, a2, a3, which, z, block):
    rows = []
    for dt, dz, dy, dx in OFFSETS[which]:
        at = 7 + dx + 16 * block
        rows.append(
            jnp.concatenate(
                [s[dt, z + dz, dy, at : at + 8], s[dt, z + dz, dy, at + 8 : at + 16]], axis=1
            )
        )
    rows.append(jnp.ones((24, 256), F32))
    rows.append(jnp.zeros((16, 256), F32))
    taps = jnp.concatenate(rows, axis=0).astype(BF16)
    first = jnp.dot(a1[which], taps, preferred_element_type=F32)
    first = jnp.maximum(first, 0.0).astype(BF16)
    w = a3[which]
    w = jnp.concatenate([w, w], axis=1)
    sums = []
    for half in range(2):
        second = jnp.dot(
            a2[which], first[half * 256 : half * 256 + 256], preferred_element_type=F32
        )
        second = jnp.maximum(second, 0.0) * w
        total = jnp.sum(second.reshape(32, 8, 256), axis=0)
        sums.append(total + pltpu.roll(total, 4, 0))
    return jnp.where(iota((8, 256), 0) < 4, sums[0], sums[1])


def xy_kernel(s, a1, a2, a3, out):
    def step(i, carry):
        for z in (2 * i, 2 * i + 1):
            for block in range(8):
                got = corrected(s, a1, a2, a3, 0, z, block)
                out[2 * block, z] = got[:, :128]
                out[2 * block + 1, z] = got[:, 128:]
        return carry

    lax.fori_loop(0, 2, step, 0)


def rest_kernel(core, parity, vol, near, next_, xy, a1, a2, a3, s_in, cons, s):
    c, odd = core[0], parity[0]
    for i, t in enumerate((1, 2 - 2 * c, 2 * c)):
        spread_plane(s, t, 5 - 5 * odd, near[i])
        spread_plane(s, t, 5 * odd, next_[i])

    def step(z, carry):
        for block in range(8):
            got = corrected(s, a1, a2, a3, 1, z, block)
            got = got + corrected(s, a1, a2, a3, 2, z, block)
            for j in range(2):
                at = 2 * block + j
                total = xy[at, z] + got[:, 128 * j : 128 * j + 128]
                cons[at, z] = vol[z, 8 * at : 8 * at + 8] + total / 3.0
        return carry

    lax.fori_loop(0, 4, step, 0)


def transpose_kernel(core, own, pair, out):
    c = core[0]

    def step(j, carry):
        rays = pl.ds(pl.multiple_of(256 * j, 256), 256)
        out[j, c] = own[rays, :].T
        out[j, 1 - c] = pair[rays, :].T
        return carry

    lax.fori_loop(0, 8, step, 0)


def project_kernel(blocks, pixels, out, cons, image, turned, held, sems):
    copies = [pltpu.make_async_copy(pixels.at[j], held.at[j], sems.at[j]) for j in range(8)]
    for copy in copies:
        copy.start()
    for z in range(4):
        for x in range(8):
            got = blocks[pl.ds(z * 8 + x, 16, stride=32), :]
            cons[z * 8 + x] = got
            image[16 * z : 16 * z + 16, 128 * x : 128 * x + 128] = got.astype(BF16)
    for j in range(8):
        copies[j].wait()
        got = jnp.dot(image[:, 0:512], held[j, 0], preferred_element_type=F32)
        got = got + jnp.dot(image[:, 512:1024], held[j, 1], preferred_element_type=F32)
        for z in range(4):
            for n in range(2):
                turned[2 * (j % 4) + n, pl.ds(z * 2 + j // 4, 16, stride=8), :] = got[
                    16 * z : 16 * z + 16, 128 * n : 128 * n + 128
                ]
    for n in range(8):
        lanes = slice(128 * n, 128 * n + 128)
        for t in range(16):
            out[t, :, lanes] = turned[n, 8 * t : 8 * t + 8].astype(BF16)


def misfit_kernel(parts, measured, out):
    total = parts[0].astype(F32)
    for t in range(1, 16):
        total = total + parts[t].astype(F32)
    misfit = (total - measured[...]).astype(BF16)
    for t in range(16):
        out[t] = misfit


def far_kernel(core, misfit, pair, cons, far, rows, turned, held, sems):
    copies = [
        pltpu.make_async_copy(pair.at[pl.ds(512 * j, 512)], held.at[j], sems.at[j])
        for j in range(4)
    ]
    for copy in copies:
        copy.start()
    for n in range(8):
        for t in range(16):
            turned[n, 8 * t : 8 * t + 8] = misfit[t, :, 128 * n : 128 * n + 128].astype(F32)
    for z in range(4):
        for half in range(2):
            for n in range(8):
                rows[16 * z : 16 * z + 16, 1024 * half + 128 * n : 1024 * half + 128 * n + 128] = (
                    turned[n, pl.ds(z * 2 + half, 16, stride=8), :].astype(BF16)
                )
    got = jnp.zeros((64, 512), F32)
    for j in range(4):
        copies[j].wait()
        left = rows[:, 512 * j : 512 * j + 512]
        got = got + jnp.dot(left, held[j], preferred_element_type=F32)
    stepped(1 - core[0], cons, got, far)


def stepped(c, cons, gradient, out):
    for z in range(4):
        for x in range(4):
            at = (slice(16 * z, 16 * z + 16), slice(128 * x, 128 * x + 128))
            out[at] = cons[z * 8 + x + 4 * c] - gradient[at]


def near_kernel(core, rows, own, cons, near):
    got = jnp.dot(rows[...], own[...], preferred_element_type=F32)
    stepped(core[0], cons, got, near)


def merge_kernel(core, near, far, out, turned):
    def write(parity, rows):
        for z in range(4):
            for x in range(4):
                turned[x, pl.ds(4 * parity + z, 16, stride=8), :] = rows[
                    16 * z : 16 * z + 16, 128 * x : 128 * x + 128
                ]

    @pl.when(core[0] == 0)
    def _():
        write(0, near)
        write(1, far)

    @pl.when(core[0] == 1)
    def _():
        write(1, near)
        write(0, far)

    for x in range(4):
        for t in range(32):
            out[t, :, 128 * x : 128 * x + 128] = turned[x, 4 * t : 4 * t + 4]


def shards(volume, lift_weights, lift_bias, mix_weights, out_weights, projector, measured):
    core = lax.axis_index("c").reshape(1)
    parity = (lax.axis_index("space") & 1).reshape(1)
    coarse = volume[0].astype(BF16)
    near = lax.ppermute(coarse, "c", SWAP)
    up = [(2 * i + 1, 2 * i + 2) for i in range(15)]
    next_ = lax.ppermute(coarse, ("q", "c"), up + [(j, i) for i, j in up])
    pair = lax.ppermute(projector, "c", SWAP)

    a1, a2, a3 = call(
        weights_kernel,
        (shaped((3, 512, 256), BF16), shaped((3, 256, 256), BF16), shaped((3, 256, 128), F32)),
        specs=[VM] * 2,
        flops=10**8,
        nbytes=1 << 20,
    )(
        jnp.concatenate([mix_weights, lift_weights.transpose(0, 2, 1)], axis=1),
        jnp.stack([lift_bias, out_weights.astype(F32)]),
    )
    planes, plane = shaped((3, 6, 3, 144, 128), F32), shaped((3, 128, 128), BF16)
    s, to_near, to_next = call(
        spread_kernel, (planes, plane, plane), specs=[SM] * 2 + [VM] * 3, nbytes=8 << 20
    )(core, parity, coarse, near, next_)
    z_near = lax.ppermute(to_near, "space", [(i, i ^ 1) for i in range(8)])
    up = [(2 * i + 1, 2 * i + 2) for i in range(3)]
    z_next = lax.ppermute(to_next, "space", up + [(j, i) for i, j in up])

    blocks = shaped((16, 4, 8, 128), F32)
    xy = call(xy_kernel, blocks, specs=[VM] * 4, flops=12 * 10**9, nbytes=1 << 20)(s, a1, a2, a3)
    consensus, _ = call(
        rest_kernel,
        (blocks, planes),
        specs=[SM] * 2 + [VM] * 8,
        flops=24 * 10**9,
        nbytes=1 << 20,
        aliases={9: 1},
    )(core, parity, volume[0], z_near, z_next, xy, a1, a2, a3, s)
    frames = lax.all_to_all(
        consensus.reshape(16, 32, 128), "q", split_axis=0, concat_axis=0, tiled=True
    )
    pixels = call(
        transpose_kernel,
        shaped((8, 2, 512, 256), BF16),
        specs=[SM, VM, VM],
        nbytes=8 << 20,
    )(core, projector, pair)

    partial, cons = call(
        project_kernel,
        (shaped((16, 8, 1024), BF16), shaped((32, 16, 128), F32)),
        [
            pltpu.VMEM((64, 1024), BF16),
            pltpu.VMEM((8, 128, 128), F32),
            pltpu.VMEM((8, 2, 512, 256), BF16),
            pltpu.SemaphoreType.DMA((8,)),
        ],
        [VM, HB],
        flops=3 * 10**8,
        nbytes=5 << 20,
        vmem=52,
    )(frames.reshape(512, 128), pixels)
    parts = lax.all_to_all(partial, "q", split_axis=0, concat_axis=0, tiled=True)
    misfit = call(misfit_kernel, shaped((16, 8, 1024), BF16), specs=[VM] * 2)(
        parts, measured.reshape(8, 1024)
    )
    misfit = lax.all_to_all(misfit, "q", split_axis=0, concat_axis=0, tiled=True)
    far, rows = call(
        far_kernel,
        (shaped((64, 512), F32), shaped((64, 2048), BF16)),
        [
            pltpu.VMEM((8, 128, 128), F32),
            pltpu.VMEM((4, 512, 512), BF16),
            pltpu.SemaphoreType.DMA((4,)),
        ],
        [SM, VM, HB, VM],
        flops=15 * 10**7,
        nbytes=3 << 20,
    )(core, misfit, pair, cons)
    far = lax.ppermute(far, "c", SWAP)
    near = call(
        near_kernel,
        shaped((64, 512), F32),
        specs=[SM] + [VM] * 3,
        flops=15 * 10**7,
        nbytes=3 << 20,
    )(core, rows, projector, cons)
    return call(
        merge_kernel,
        shaped((32, 4, 512), F32),
        [pltpu.VMEM((4, 128, 128), F32)],
        [SM] + [VM] * 2,
    )(core, near, far)


def solution(mesh):
    fine = Mesh(mesh.devices.reshape(8, 16, 2), ("space", "q", "c"))
    tm = ("q", "c")
    placed = (
        P(tm, "space", None, None),
        P(),
        P(),
        P(),
        P(),
        P(None, tm),
        P(tm, "space", None),
    )
    return jax.shard_map(
        shards, mesh=fine, in_specs=placed, out_specs=P(None, "space", tm), check_vma=False
    )
```

```python
import jax
import jax.numpy as jnp
from jax import lax
from jax.experimental import pallas as pl
from jax.experimental.pallas import tpu as pltpu
from jax.sharding import Mesh, PartitionSpec as P

F32, BF16 = jnp.float32, jnp.bfloat16
VM = pl.BlockSpec(memory_space=pltpu.VMEM)
SM = pl.BlockSpec(memory_space=pltpu.SMEM)
HB = pl.BlockSpec(memory_space=pltpu.HBM)
SWAP = [(0, 1), (1, 0)]
NT = (((1,), (1,)), ((), ()))


def call(kernel, outs, scratch=(), specs=None, flops=0, nbytes=0, vmem=24, aliases=None):
    return pl.pallas_call(
        kernel,
        out_shape=outs,
        in_specs=specs,
        out_specs=jax.tree.map(lambda _: VM, outs),
        scratch_shapes=list(scratch),
        input_output_aliases=aliases or {},
        compiler_params=pltpu.CompilerParams(vmem_limit_bytes=vmem << 20),
        cost_estimate=pl.CostEstimate(flops=flops, bytes_accessed=nbytes, transcendentals=0),
    )


def shaped(shape, dtype):
    return jax.ShapeDtypeStruct(shape, dtype)


def iota(shape, dim):
    return lax.broadcasted_iota(jnp.int32, shape, dim)


def weights_kernel(matrices, vectors, a1, a2, a3):
    spread = (iota((256, 64), 0) >> 2 == iota((256, 64), 1)).astype(F32)
    spread_t = (iota((64, 256), 1) >> 2 == iota((64, 256), 0)).astype(F32).astype(BF16)
    taps = (iota((27, 256), 1) >> 3 == iota((27, 256), 0)).astype(F32).astype(BF16)
    row, col = iota((256, 256), 0) & 3, iota((256, 256), 1)
    tap = col >> 3
    spread_b = spread.astype(BF16)

    def column(values):
        return jnp.sum(spread * values, axis=1, keepdims=True)

    for k in range(3):
        full = vectors[0, k : k + 1]
        high = full.astype(BF16).astype(F32)
        mid = (full - high).astype(BF16).astype(F32)
        low = full - high - mid
        base = lax.dot_general(spread_b, matrices[k, 64:91], NT, preferred_element_type=F32).astype(BF16)
        base = jnp.dot(base, taps, preferred_element_type=F32)
        for at, part in ((27, high), (28, mid), (29, low)):
            base = jnp.where(tap == at, column(part), base)
        for half in range(2):
            a1[k, half * 256 : half * 256 + 256] = jnp.where(
                row + 4 * half == (col & 7), base, 0.0
            ).astype(BF16)
        mixed = jnp.dot(spread_b, matrices[k, 0:64], preferred_element_type=F32).astype(BF16)
        mixed = jnp.dot(mixed, spread_t, preferred_element_type=F32)
        a2[k] = jnp.where(row == (col & 3), mixed, 0.0).astype(BF16)
        a3[k] = jnp.broadcast_to(column(vectors[1, k : k + 1]), (256, 128))


def spread_plane(s, t, z, plane):
    zero = jnp.zeros((8, 128), F32)
    lane = iota((8, 128), 1)
    for dy in range(3):
        s[t, z, dy, 0:8] = zero
        s[t, z, dy, 136:144] = zero
    for j in range(8):
        pair = plane[16 * j : 16 * j + 16].astype(F32)
        for i in range(2):
            v = pair[8 * i : 8 * i + 8]
            at = slice(16 * j + 8 * i + 8, 16 * j + 8 * i + 16)
            s[t, z, 0, at] = jnp.where(lane == 0, 0.0, pltpu.roll(v, 1, 1))
            s[t, z, 1, at] = v
            s[t, z, 2, at] = jnp.where(lane == 127, 0.0, pltpu.roll(v, 127, 1))


def spread_kernel(core, parity, mine, near, next_, s, to_near, to_next):
    c, odd = core[0], parity[0]
    for i, ref in enumerate((mine, near, next_)):
        to_near[i] = ref[3 - 3 * odd]
        to_next[i] = ref[3 * odd]

    def step(z, carry):
        spread_plane(s, 1, z + 1, mine[z])
        spread_plane(s, 2 - 2 * c, z + 1, near[z])
        spread_plane(s, 2 * c, z + 1, next_[z])
        return carry

    lax.fori_loop(0, 4, step, 0)


OFFSETS = (
    [(dt, 1, db, da) for dt in range(3) for da in range(3) for db in range(3)],
    [(dt, db, da, 1) for dt in range(3) for da in range(3) for db in range(3)],
    [(dt, da, 1, db) for dt in range(3) for da in range(3) for db in range(3)],
)


def corrected(s, a1, a2, a3, which, z, block):
    rows = []
    for dt, dz, dy, dx in OFFSETS[which]:
        at = 7 + dx + 16 * block
        rows.append(
            jnp.concatenate(
                [s[dt, z + dz, dy, at : at + 8], s[dt, z + dz, dy, at + 8 : at + 16]], axis=1
            )
        )
    rows.append(jnp.ones((24, 256), F32))
    rows.append(jnp.zeros((16, 256), F32))
    taps = jnp.concatenate(rows, axis=0).astype(BF16)
    first = jnp.dot(a1[which], taps, preferred_element_type=F32)
    first = jnp.maximum(first, 0.0).astype(BF16)
    w = a3[which]
    w = jnp.concatenate([w, w], axis=1)
    sums = []
    for half in range(2):
        second = jnp.dot(
            a2[which], first[half * 256 : half * 256 + 256], preferred_element_type=F32
        )
        second = jnp.maximum(second, 0.0) * w
        total = jnp.sum(second.reshape(32, 8, 256), axis=0)
        sums.append(total + pltpu.roll(total, 4, 0))
    return jnp.where(iota((8, 256), 0) < 4, sums[0], sums[1])


def xy_kernel(s, a1, a2, a3, out):
    def step(i, carry):
        for z in (2 * i, 2 * i + 1):
            for block in range(8):
                got = corrected(s, a1, a2, a3, 0, z, block)
                out[2 * block, z] = got[:, :128]
                out[2 * block + 1, z] = got[:, 128:]
        return carry

    lax.fori_loop(0, 2, step, 0)


def rest_kernel(core, parity, vol, near, next_, xy, a1, a2, a3, s_in, cons, s):
    c, odd = core[0], parity[0]
    for i, t in enumerate((1, 2 - 2 * c, 2 * c)):
        spread_plane(s, t, 5 - 5 * odd, near[i])
        spread_plane(s, t, 5 * odd, next_[i])

    def step(z, carry):
        for block in range(8):
            got = corrected(s, a1, a2, a3, 1, z, block)
            got = got + corrected(s, a1, a2, a3, 2, z, block)
            for j in range(2):
                at = 2 * block + j
                total = xy[at, z] + got[:, 128 * j : 128 * j + 128]
                cons[at, z] = vol[z, 8 * at : 8 * at + 8] + total / 3.0
        return carry

    lax.fori_loop(0, 4, step, 0)


def transpose_kernel(block, out):
    def step(j, carry):
        out[j] = block[pl.ds(pl.multiple_of(256 * j, 256), 256), :].T
        return carry

    lax.fori_loop(0, 8, step, 0)


def project_kernel(core, blocks, own, pair, out, cons, image, turned, held, sems):
    copies = [
        pltpu.make_async_copy((own, pair)[i % 2].at[i // 2], held.at[i], sems.at[i])
        for i in range(16)
    ]
    for copy in copies[:4]:
        copy.start()
    for z in range(4):
        for x in range(8):
            got = blocks[pl.ds(z * 8 + x, 16, stride=32), :]
            cons[z * 8 + x] = got
            at = (slice(16 * z, 16 * z + 16), slice(128 * (x % 4), 128 * (x % 4) + 128))
            image[x // 4, at[0], at[1]] = got.astype(BF16)
    c = core[0]
    mine, theirs = image[c], image[1 - c]
    for j in range(8):
        for i in (2 * j, 2 * j + 1):
            if i + 4 < 16:
                copies[i + 4].start()
            copies[i].wait()
        got = jnp.dot(mine, held[2 * j], preferred_element_type=F32)
        got = got + jnp.dot(theirs, held[2 * j + 1], preferred_element_type=F32)
        for z in range(4):
            for n in range(2):
                turned[2 * (j % 4) + n, pl.ds(z * 2 + j // 4, 16, stride=8), :] = got[
                    16 * z : 16 * z + 16, 128 * n : 128 * n + 128
                ]
    for n in range(8):
        lanes = slice(128 * n, 128 * n + 128)
        for t in range(16):
            out[t, :, lanes] = turned[n, 8 * t : 8 * t + 8].astype(BF16)


def misfit_kernel(parts, measured, out):
    total = parts[0].astype(F32)
    for t in range(1, 16):
        total = total + parts[t].astype(F32)
    misfit = (total - measured[...]).astype(BF16)
    for t in range(16):
        out[t] = misfit


def far_kernel(core, misfit, pair, cons, far, rows, turned, held, sems):
    copies = [
        pltpu.make_async_copy(pair.at[pl.ds(512 * j, 512)], held.at[j], sems.at[j])
        for j in range(4)
    ]
    for copy in copies:
        copy.start()
    for n in range(8):
        for t in range(16):
            turned[n, 8 * t : 8 * t + 8] = misfit[t, :, 128 * n : 128 * n + 128].astype(F32)
    for z in range(4):
        for half in range(2):
            for n in range(8):
                rows[16 * z : 16 * z + 16, 1024 * half + 128 * n : 1024 * half + 128 * n + 128] = (
                    turned[n, pl.ds(z * 2 + half, 16, stride=8), :].astype(BF16)
                )
    got = jnp.zeros((64, 512), F32)
    for j in range(4):
        copies[j].wait()
        left = rows[:, 512 * j : 512 * j + 512]
        got = got + jnp.dot(left, held[j], preferred_element_type=F32)
    stepped(1 - core[0], cons, got, far)


def stepped(c, cons, gradient, out):
    for z in range(4):
        for x in range(4):
            at = (slice(16 * z, 16 * z + 16), slice(128 * x, 128 * x + 128))
            out[at] = cons[z * 8 + x + 4 * c] - gradient[at]


def near_kernel(core, rows, own, cons, near):
    got = jnp.dot(rows[...], own[...], preferred_element_type=F32)
    stepped(core[0], cons, got, near)


def merge_kernel(core, near, far, out, turned):
    def write(parity, rows):
        for z in range(4):
            for x in range(4):
                turned[x, pl.ds(4 * parity + z, 16, stride=8), :] = rows[
                    16 * z : 16 * z + 16, 128 * x : 128 * x + 128
                ]

    @pl.when(core[0] == 0)
    def _():
        write(0, near)
        write(1, far)

    @pl.when(core[0] == 1)
    def _():
        write(1, near)
        write(0, far)

    for x in range(4):
        for t in range(32):
            out[t, :, 128 * x : 128 * x + 128] = turned[x, 4 * t : 4 * t + 4]


def shards(volume, lift_weights, lift_bias, mix_weights, out_weights, projector, measured):
    core = lax.axis_index("c").reshape(1)
    parity = (lax.axis_index("space") & 1).reshape(1)
    coarse = volume[0].astype(BF16)
    near = lax.ppermute(coarse, "c", SWAP)
    up = [(2 * i + 1, 2 * i + 2) for i in range(15)]
    next_ = lax.ppermute(coarse, ("q", "c"), up + [(j, i) for i, j in up])
    a1, a2, a3 = call(
        weights_kernel,
        (shaped((3, 512, 256), BF16), shaped((3, 256, 256), BF16), shaped((3, 256, 128), F32)),
        specs=[VM] * 2,
        flops=10**8,
        nbytes=1 << 20,
    )(
        jnp.concatenate([mix_weights, lift_weights.transpose(0, 2, 1)], axis=1),
        jnp.stack([lift_bias, out_weights.astype(F32)]),
    )
    planes, plane = shaped((3, 6, 3, 144, 128), F32), shaped((3, 128, 128), BF16)
    s, to_near, to_next = call(
        spread_kernel, (planes, plane, plane), specs=[SM] * 2 + [VM] * 3, nbytes=8 << 20
    )(core, parity, coarse, near, next_)
    to_near, later = lax.optimization_barrier((to_near, projector))
    z_near = lax.ppermute(to_near, "space", [(i, i ^ 1) for i in range(8)])
    up = [(2 * i + 1, 2 * i + 2) for i in range(3)]
    z_next = lax.ppermute(to_next, "space", up + [(j, i) for i, j in up])

    pair = lax.ppermute(later, "c", SWAP)
    blocks = shaped((16, 4, 8, 128), F32)
    xy = call(xy_kernel, blocks, specs=[VM] * 4, flops=12 * 10**9, nbytes=1 << 20)(s, a1, a2, a3)
    consensus, _ = call(
        rest_kernel,
        (blocks, planes),
        specs=[SM] * 2 + [VM] * 8,
        flops=24 * 10**9,
        nbytes=1 << 20,
        aliases={9: 1},
    )(core, parity, volume[0], z_near, z_next, xy, a1, a2, a3, s)
    frames = lax.all_to_all(
        consensus.reshape(16, 32, 128), "q", split_axis=0, concat_axis=0, tiled=True
    )
    turned = [
        call(transpose_kernel, shaped((8, 512, 256), BF16), specs=[VM], nbytes=4 << 20)(block)
        for block in (pair, projector)
    ]

    partial, cons = call(
        project_kernel,
        (shaped((16, 8, 1024), BF16), shaped((32, 16, 128), F32)),
        [
            pltpu.VMEM((2, 64, 512), BF16),
            pltpu.VMEM((8, 128, 128), F32),
            pltpu.VMEM((16, 512, 256), BF16),
            pltpu.SemaphoreType.DMA((16,)),
        ],
        [SM, VM, HB, HB],
        flops=3 * 10**8,
        nbytes=5 << 20,
        vmem=52,
    )(core, frames.reshape(512, 128), turned[1], turned[0])
    parts = lax.all_to_all(partial, "q", split_axis=0, concat_axis=0, tiled=True)
    misfit = call(misfit_kernel, shaped((16, 8, 1024), BF16), specs=[VM] * 2)(
        parts, measured.reshape(8, 1024)
    )
    misfit = lax.all_to_all(misfit, "q", split_axis=0, concat_axis=0, tiled=True)
    far, rows = call(
        far_kernel,
        (shaped((64, 512), F32), shaped((64, 2048), BF16)),
        [
            pltpu.VMEM((8, 128, 128), F32),
            pltpu.VMEM((4, 512, 512), BF16),
            pltpu.SemaphoreType.DMA((4,)),
        ],
        [SM, VM, HB, VM],
        flops=15 * 10**7,
        nbytes=3 << 20,
    )(core, misfit, pair, cons)
    far = lax.ppermute(far, "c", SWAP)
    near = call(
        near_kernel,
        shaped((64, 512), F32),
        specs=[SM] + [VM] * 3,
        flops=15 * 10**7,
        nbytes=3 << 20,
    )(core, rows, projector, cons)
    return call(
        merge_kernel,
        shaped((32, 4, 512), F32),
        [pltpu.VMEM((4, 128, 128), F32)],
        [SM] + [VM] * 2,
    )(core, near, far)


def solution(mesh):
    fine = Mesh(mesh.devices.reshape(8, 16, 2), ("space", "q", "c"))
    tm = ("q", "c")
    placed = (
        P(tm, "space", None, None),
        P(),
        P(),
        P(),
        P(),
        P(None, tm),
        P(tm, "space", None),
    )
    return jax.shard_map(
        shards, mesh=fine, in_specs=placed, out_specs=P(None, "space", tm), check_vma=False
    )
```

```python
import jax
import jax.numpy as jnp
from jax import lax
from jax.experimental import pallas as pl
from jax.experimental.pallas import tpu as pltpu
from jax.sharding import Mesh, PartitionSpec as P

F32, BF16 = jnp.float32, jnp.bfloat16
VM = pl.BlockSpec(memory_space=pltpu.VMEM)
SM = pl.BlockSpec(memory_space=pltpu.SMEM)
HB = pl.BlockSpec(memory_space=pltpu.HBM)
SWAP = [(0, 1), (1, 0)]
NT = (((1,), (1,)), ((), ()))


def call(kernel, outs, scratch=(), specs=None, flops=0, nbytes=0, vmem=24, aliases=None):
    return pl.pallas_call(
        kernel,
        out_shape=outs,
        in_specs=specs,
        out_specs=jax.tree.map(lambda _: VM, outs),
        scratch_shapes=list(scratch),
        input_output_aliases=aliases or {},
        compiler_params=pltpu.CompilerParams(vmem_limit_bytes=vmem << 20),
        cost_estimate=pl.CostEstimate(flops=flops, bytes_accessed=nbytes, transcendentals=0),
    )


def shaped(shape, dtype):
    return jax.ShapeDtypeStruct(shape, dtype)


def iota(shape, dim):
    return lax.broadcasted_iota(jnp.int32, shape, dim)


def weights_kernel(matrices, vectors, a1, a2, a3):
    spread = (iota((256, 64), 0) >> 2 == iota((256, 64), 1)).astype(F32)
    spread_t = (iota((64, 256), 1) >> 2 == iota((64, 256), 0)).astype(F32).astype(BF16)
    taps = (iota((27, 256), 1) >> 3 == iota((27, 256), 0)).astype(F32).astype(BF16)
    row, col = iota((256, 256), 0) & 3, iota((256, 256), 1)
    tap = col >> 3
    spread_b = spread.astype(BF16)

    def column(values):
        return jnp.sum(spread * values, axis=1, keepdims=True)

    for k in range(3):
        full = vectors[0, k : k + 1]
        high = full.astype(BF16).astype(F32)
        mid = (full - high).astype(BF16).astype(F32)
        low = full - high - mid
        base = lax.dot_general(spread_b, matrices[k, 64:91], NT, preferred_element_type=F32).astype(BF16)
        base = jnp.dot(base, taps, preferred_element_type=F32)
        for at, part in ((27, high), (28, mid), (29, low)):
            base = jnp.where(tap == at, column(part), base)
        for half in range(2):
            a1[k, half * 256 : half * 256 + 256] = jnp.where(
                row + 4 * half == (col & 7), base, 0.0
            ).astype(BF16)
        mixed = jnp.dot(spread_b, matrices[k, 0:64], preferred_element_type=F32).astype(BF16)
        mixed = jnp.dot(mixed, spread_t, preferred_element_type=F32)
        a2[k] = jnp.where(row == (col & 3), mixed, 0.0).astype(BF16)
        a3[k] = jnp.broadcast_to(column(vectors[1, k : k + 1]), (256, 128))


def spread_plane(s, t, z, plane):
    zero = jnp.zeros((8, 128), F32)
    lane = iota((8, 128), 1)
    for dy in range(3):
        s[t, z, dy, 0:8] = zero
        s[t, z, dy, 136:144] = zero
    for j in range(8):
        pair = plane[16 * j : 16 * j + 16].astype(F32)
        for i in range(2):
            v = pair[8 * i : 8 * i + 8]
            at = slice(16 * j + 8 * i + 8, 16 * j + 8 * i + 16)
            s[t, z, 0, at] = jnp.where(lane == 0, 0.0, pltpu.roll(v, 1, 1))
            s[t, z, 1, at] = v
            s[t, z, 2, at] = jnp.where(lane == 127, 0.0, pltpu.roll(v, 127, 1))


def spread_kernel(core, parity, mine, near, next_, s, to_near, to_next):
    c, odd = core[0], parity[0]
    for i, ref in enumerate((mine, near, next_)):
        to_near[i] = ref[3 - 3 * odd]
        to_next[i] = ref[3 * odd]

    def step(z, carry):
        spread_plane(s, 1, z + 1, mine[z])
        spread_plane(s, 2 - 2 * c, z + 1, near[z])
        spread_plane(s, 2 * c, z + 1, next_[z])
        return carry

    lax.fori_loop(0, 4, step, 0)


OFFSETS = (
    [(dt, 1, db, da) for dt in range(3) for da in range(3) for db in range(3)],
    [(dt, db, da, 1) for dt in range(3) for da in range(3) for db in range(3)],
    [(dt, da, 1, db) for dt in range(3) for da in range(3) for db in range(3)],
)


def corrected(s, a1, a2, a3, which, z, block):
    rows = []
    for dt, dz, dy, dx in OFFSETS[which]:
        at = 7 + dx + 16 * block
        rows.append(
            jnp.concatenate(
                [s[dt, z + dz, dy, at : at + 8], s[dt, z + dz, dy, at + 8 : at + 16]], axis=1
            )
        )
    rows.append(jnp.ones((24, 256), F32))
    rows.append(jnp.zeros((16, 256), F32))
    taps = jnp.concatenate(rows, axis=0).astype(BF16)
    first = jnp.dot(a1[which], taps, preferred_element_type=F32)
    first = jnp.maximum(first, 0.0).astype(BF16)
    w = a3[which]
    w = jnp.concatenate([w, w], axis=1)
    sums = []
    for half in range(2):
        second = jnp.dot(
            a2[which], first[half * 256 : half * 256 + 256], preferred_element_type=F32
        )
        second = jnp.maximum(second, 0.0) * w
        total = jnp.sum(second.reshape(32, 8, 256), axis=0)
        sums.append(total + pltpu.roll(total, 4, 0))
    return jnp.where(iota((8, 256), 0) < 4, sums[0], sums[1])


def xy_kernel(s, a1, a2, a3, out):
    for z in range(4):
        for block in range(8):
            got = corrected(s, a1, a2, a3, 0, z, block)
            out[2 * block, z] = got[:, :128]
            out[2 * block + 1, z] = got[:, 128:]


def rest_kernel(core, parity, vol, near, next_, xy, a1, a2, a3, s_in, cons, s):
    c, odd = core[0], parity[0]
    for i, t in enumerate((1, 2 - 2 * c, 2 * c)):
        spread_plane(s, t, 5 - 5 * odd, near[i])
        spread_plane(s, t, 5 * odd, next_[i])

    def step(i, carry):
        for z in (2 * i, 2 * i + 1):
            for block in range(8):
                got = corrected(s, a1, a2, a3, 1, z, block)
                got = got + corrected(s, a1, a2, a3, 2, z, block)
                for j in range(2):
                    at = 2 * block + j
                    total = xy[at, z] + got[:, 128 * j : 128 * j + 128]
                    cons[at, z] = vol[z, 8 * at : 8 * at + 8] + total / 3.0
        return carry

    lax.fori_loop(0, 2, step, 0)


def transpose_kernel(block, out):
    def step(j, carry):
        out[j] = block[pl.ds(pl.multiple_of(256 * j, 256), 256), :].T
        return carry

    lax.fori_loop(0, 8, step, 0)


def project_kernel(core, blocks, own, pair, out, cons, image, turned, part, held, sems):
    copies = [pltpu.make_async_copy(pair.at[j], held.at[j], sems.at[j]) for j in range(8)]
    for copy in copies:
        copy.start()
    for z in range(4):
        for x in range(8):
            got = blocks[pl.ds(z * 8 + x, 16, stride=32), :]
            cons[z * 8 + x] = got
            lanes = slice(128 * (x % 4), 128 * (x % 4) + 128)
            image[x // 4, 16 * z : 16 * z + 16, lanes] = got.astype(BF16)
    c = core[0]
    mine, theirs = image[c], image[1 - c]
    for j in range(8):
        rays = slice(256 * j, 256 * j + 256)
        part[j] = lax.dot_general(mine, own[rays], NT, preferred_element_type=F32)
    for j in range(8):
        copies[j].wait()
        got = part[j] + jnp.dot(theirs, held[j], preferred_element_type=F32)
        for z in range(4):
            for n in range(2):
                turned[2 * (j % 4) + n, pl.ds(z * 2 + j // 4, 16, stride=8), :] = got[
                    16 * z : 16 * z + 16, 128 * n : 128 * n + 128
                ]
    for n in range(8):
        lanes = slice(128 * n, 128 * n + 128)
        for t in range(16):
            out[t, :, lanes] = turned[n, 8 * t : 8 * t + 8].astype(BF16)


def misfit_kernel(parts, measured, out):
    total = parts[0].astype(F32)
    for t in range(1, 16):
        total = total + parts[t].astype(F32)
    misfit = (total - measured[...]).astype(BF16)
    for t in range(16):
        out[t] = misfit


def far_kernel(core, misfit, pair, cons, far, rows, turned, held, sems):
    copies = [
        pltpu.make_async_copy(pair.at[pl.ds(512 * j, 512)], held.at[j], sems.at[j])
        for j in range(4)
    ]
    for copy in copies:
        copy.start()
    for n in range(8):
        for t in range(16):
            turned[n, 8 * t : 8 * t + 8] = misfit[t, :, 128 * n : 128 * n + 128].astype(F32)
    for z in range(4):
        for half in range(2):
            for n in range(8):
                rows[16 * z : 16 * z + 16, 1024 * half + 128 * n : 1024 * half + 128 * n + 128] = (
                    turned[n, pl.ds(z * 2 + half, 16, stride=8), :].astype(BF16)
                )
    got = jnp.zeros((64, 512), F32)
    for j in range(4):
        copies[j].wait()
        left = rows[:, 512 * j : 512 * j + 512]
        got = got + jnp.dot(left, held[j], preferred_element_type=F32)
    stepped(1 - core[0], cons, got, far)


def stepped(c, cons, gradient, out):
    for z in range(4):
        for x in range(4):
            at = (slice(16 * z, 16 * z + 16), slice(128 * x, 128 * x + 128))
            out[at] = cons[z * 8 + x + 4 * c] - gradient[at]


def near_kernel(core, rows, own, cons, near):
    got = jnp.dot(rows[...], own[...], preferred_element_type=F32)
    stepped(core[0], cons, got, near)


def merge_kernel(core, near, far, out, turned):
    def write(parity, rows):
        for z in range(4):
            for x in range(4):
                turned[x, pl.ds(4 * parity + z, 16, stride=8), :] = rows[
                    16 * z : 16 * z + 16, 128 * x : 128 * x + 128
                ]

    @pl.when(core[0] == 0)
    def _():
        write(0, near)
        write(1, far)

    @pl.when(core[0] == 1)
    def _():
        write(1, near)
        write(0, far)

    for x in range(4):
        for t in range(32):
            out[t, :, 128 * x : 128 * x + 128] = turned[x, 4 * t : 4 * t + 4]


def shards(volume, lift_weights, lift_bias, mix_weights, out_weights, projector, measured):
    core = lax.axis_index("c").reshape(1)
    parity = (lax.axis_index("space") & 1).reshape(1)
    coarse = volume[0].astype(BF16)
    near = lax.ppermute(coarse, "c", SWAP)
    up = [(2 * i + 1, 2 * i + 2) for i in range(15)]
    next_ = lax.ppermute(coarse, ("q", "c"), up + [(j, i) for i, j in up])
    pair = lax.ppermute(projector, "c", SWAP)

    a1, a2, a3 = call(
        weights_kernel,
        (shaped((3, 512, 256), BF16), shaped((3, 256, 256), BF16), shaped((3, 256, 128), F32)),
        specs=[VM] * 2,
        flops=10**8,
        nbytes=1 << 20,
    )(
        jnp.concatenate([mix_weights, lift_weights.transpose(0, 2, 1)], axis=1),
        jnp.stack([lift_bias, out_weights.astype(F32)]),
    )
    planes, plane = shaped((3, 6, 3, 144, 128), F32), shaped((3, 128, 128), BF16)
    s, to_near, to_next = call(
        spread_kernel, (planes, plane, plane), specs=[SM] * 2 + [VM] * 3, nbytes=8 << 20
    )(core, parity, coarse, near, next_)
    z_near = lax.ppermute(to_near, "space", [(i, i ^ 1) for i in range(8)])
    up = [(2 * i + 1, 2 * i + 2) for i in range(3)]
    z_next = lax.ppermute(to_next, "space", up + [(j, i) for i, j in up])

    blocks = shaped((16, 4, 8, 128), F32)
    xy = call(xy_kernel, blocks, specs=[VM] * 4, flops=12 * 10**9, nbytes=1 << 20)(s, a1, a2, a3)
    consensus, _ = call(
        rest_kernel,
        (blocks, planes),
        specs=[SM] * 2 + [VM] * 8,
        flops=24 * 10**9,
        nbytes=1 << 20,
        aliases={9: 1},
    )(core, parity, volume[0], z_near, z_next, xy, a1, a2, a3, s)
    frames = lax.all_to_all(
        consensus.reshape(16, 32, 128), "q", split_axis=0, concat_axis=0, tiled=True
    )
    turned = call(transpose_kernel, shaped((8, 512, 256), BF16), specs=[VM], nbytes=4 << 20)(pair)

    partial, cons = call(
        project_kernel,
        (shaped((16, 8, 1024), BF16), shaped((32, 16, 128), F32)),
        [
            pltpu.VMEM((2, 64, 512), BF16),
            pltpu.VMEM((8, 128, 128), F32),
            pltpu.VMEM((8, 64, 256), F32),
            pltpu.VMEM((8, 512, 256), BF16),
            pltpu.SemaphoreType.DMA((8,)),
        ],
        [SM, VM, VM, HB],
        flops=3 * 10**8,
        nbytes=5 << 20,
        vmem=48,
    )(core, frames.reshape(512, 128), projector, turned)
    parts = lax.all_to_all(partial, "q", split_axis=0, concat_axis=0, tiled=True)
    misfit = call(misfit_kernel, shaped((16, 8, 1024), BF16), specs=[VM] * 2)(
        parts, measured.reshape(8, 1024)
    )
    misfit = lax.all_to_all(misfit, "q", split_axis=0, concat_axis=0, tiled=True)
    far, rows = call(
        far_kernel,
        (shaped((64, 512), F32), shaped((64, 2048), BF16)),
        [
            pltpu.VMEM((8, 128, 128), F32),
            pltpu.VMEM((4, 512, 512), BF16),
            pltpu.SemaphoreType.DMA((4,)),
        ],
        [SM, VM, HB, VM],
        flops=15 * 10**7,
        nbytes=3 << 20,
    )(core, misfit, pair, cons)
    far = lax.ppermute(far, "c", SWAP)
    near = call(
        near_kernel,
        shaped((64, 512), F32),
        specs=[SM] + [VM] * 3,
        flops=15 * 10**7,
        nbytes=3 << 20,
    )(core, rows, projector, cons)
    return call(
        merge_kernel,
        shaped((32, 4, 512), F32),
        [pltpu.VMEM((4, 128, 128), F32)],
        [SM] + [VM] * 2,
    )(core, near, far)


def solution(mesh):
    fine = Mesh(mesh.devices.reshape(8, 16, 2), ("space", "q", "c"))
    tm = ("q", "c")
    placed = (
        P(tm, "space", None, None),
        P(),
        P(),
        P(),
        P(),
        P(None, tm),
        P(tm, "space", None),
    )
    return jax.shard_map(
        shards, mesh=fine, in_specs=placed, out_specs=P(None, "space", tm), check_vma=False
    )
```

```python
import jax
import jax.numpy as jnp
from jax import lax
from jax.experimental import pallas as pl
from jax.experimental.pallas import tpu as pltpu
from jax.sharding import Mesh, PartitionSpec as P

F32, BF16 = jnp.float32, jnp.bfloat16
VM = pl.BlockSpec(memory_space=pltpu.VMEM)
SM = pl.BlockSpec(memory_space=pltpu.SMEM)
HB = pl.BlockSpec(memory_space=pltpu.HBM)
SWAP = [(0, 1), (1, 0)]
NT = (((1,), (1,)), ((), ()))


def call(kernel, outs, scratch=(), specs=None, flops=0, nbytes=0, vmem=24, aliases=None):
    return pl.pallas_call(
        kernel,
        out_shape=outs,
        in_specs=specs,
        out_specs=jax.tree.map(lambda _: VM, outs),
        scratch_shapes=list(scratch),
        input_output_aliases=aliases or {},
        compiler_params=pltpu.CompilerParams(vmem_limit_bytes=vmem << 20),
        cost_estimate=pl.CostEstimate(flops=flops, bytes_accessed=nbytes, transcendentals=0),
    )


def shaped(shape, dtype):
    return jax.ShapeDtypeStruct(shape, dtype)


def iota(shape, dim):
    return lax.broadcasted_iota(jnp.int32, shape, dim)


def weights_kernel(matrices, vectors, a1, a2, a3):
    spread = (iota((256, 64), 0) >> 2 == iota((256, 64), 1)).astype(F32)
    spread_t = (iota((64, 256), 1) >> 2 == iota((64, 256), 0)).astype(F32).astype(BF16)
    taps = (iota((27, 256), 1) >> 3 == iota((27, 256), 0)).astype(F32).astype(BF16)
    row, col = iota((256, 256), 0) & 3, iota((256, 256), 1)
    tap = col >> 3
    spread_b = spread.astype(BF16)

    def column(values):
        return jnp.sum(spread * values, axis=1, keepdims=True)

    for k in range(3):
        full = vectors[0, k : k + 1]
        high = full.astype(BF16).astype(F32)
        mid = (full - high).astype(BF16).astype(F32)
        low = full - high - mid
        base = lax.dot_general(spread_b, matrices[k, 64:91], NT, preferred_element_type=F32).astype(BF16)
        base = jnp.dot(base, taps, preferred_element_type=F32)
        for at, part in ((27, high), (28, mid), (29, low)):
            base = jnp.where(tap == at, column(part), base)
        for half in range(2):
            a1[k, half * 256 : half * 256 + 256] = jnp.where(
                row + 4 * half == (col & 7), base, 0.0
            ).astype(BF16)
        mixed = jnp.dot(spread_b, matrices[k, 0:64], preferred_element_type=F32).astype(BF16)
        mixed = jnp.dot(mixed, spread_t, preferred_element_type=F32)
        a2[k] = jnp.where(row == (col & 3), mixed, 0.0).astype(BF16)
        a3[k] = jnp.broadcast_to(column(vectors[1, k : k + 1]), (256, 128))


def spread_plane(s, t, z, plane):
    zero = jnp.zeros((8, 128), F32)
    lane = iota((8, 128), 1)
    for dy in range(3):
        s[t, z, dy, 0:8] = zero
        s[t, z, dy, 136:144] = zero
    for j in range(8):
        pair = plane[16 * j : 16 * j + 16].astype(F32)
        for i in range(2):
            v = pair[8 * i : 8 * i + 8]
            at = slice(16 * j + 8 * i + 8, 16 * j + 8 * i + 16)
            s[t, z, 0, at] = jnp.where(lane == 0, 0.0, pltpu.roll(v, 1, 1))
            s[t, z, 1, at] = v
            s[t, z, 2, at] = jnp.where(lane == 127, 0.0, pltpu.roll(v, 127, 1))


def spread_kernel(core, parity, mine, near, next_, s, to_near, to_next):
    c, odd = core[0], parity[0]
    for i, ref in enumerate((mine, near, next_)):
        to_near[i] = ref[3 - 3 * odd]
        to_next[i] = ref[3 * odd]

    def step(z, carry):
        spread_plane(s, 1, z + 1, mine[z])
        spread_plane(s, 2 - 2 * c, z + 1, near[z])
        spread_plane(s, 2 * c, z + 1, next_[z])
        return carry

    lax.fori_loop(0, 4, step, 0)


OFFSETS = (
    [(dt, 1, db, da) for dt in range(3) for da in range(3) for db in range(3)],
    [(dt, db, da, 1) for dt in range(3) for da in range(3) for db in range(3)],
    [(dt, da, 1, db) for dt in range(3) for da in range(3) for db in range(3)],
)


def corrected(s, a1, a2, a3, which, z, block):
    rows = []
    for dt, dz, dy, dx in OFFSETS[which]:
        at = 7 + dx + 16 * block
        rows.append(
            jnp.concatenate(
                [s[dt, z + dz, dy, at : at + 8], s[dt, z + dz, dy, at + 8 : at + 16]], axis=1
            )
        )
    rows.append(jnp.ones((24, 256), F32))
    rows.append(jnp.zeros((16, 256), F32))
    taps = jnp.concatenate(rows, axis=0).astype(BF16)
    first = jnp.dot(a1[which], taps, preferred_element_type=F32)
    first = jnp.maximum(first, 0.0).astype(BF16)
    w = a3[which]
    w = jnp.concatenate([w, w], axis=1)
    sums = []
    for half in range(2):
        second = jnp.dot(
            a2[which], first[half * 256 : half * 256 + 256], preferred_element_type=F32
        )
        second = jnp.maximum(second, 0.0) * w
        total = jnp.sum(second.reshape(32, 8, 256), axis=0)
        sums.append(total + pltpu.roll(total, 4, 0))
    return jnp.where(iota((8, 256), 0) < 4, sums[0], sums[1])


def xy_kernel(s, a1, a2, a3, out):
    for z in range(4):
        for block in range(8):
            got = corrected(s, a1, a2, a3, 0, z, block)
            out[2 * block, z] = got[:, :128]
            out[2 * block + 1, z] = got[:, 128:]


def rest_kernel(core, parity, vol, near, next_, xy, a1, a2, a3, s_in, cons, s):
    c, odd = core[0], parity[0]
    for i, t in enumerate((1, 2 - 2 * c, 2 * c)):
        spread_plane(s, t, 5 - 5 * odd, near[i])
        spread_plane(s, t, 5 * odd, next_[i])

    def step(i, carry):
        for z in (2 * i, 2 * i + 1):
            for block in range(8):
                got = corrected(s, a1, a2, a3, 1, z, block)
                got = got + corrected(s, a1, a2, a3, 2, z, block)
                for j in range(2):
                    at = 2 * block + j
                    total = xy[at, z] + got[:, 128 * j : 128 * j + 128]
                    cons[at, z] = vol[z, 8 * at : 8 * at + 8] + total / 3.0
        return carry

    lax.fori_loop(0, 2, step, 0)


def transpose_kernel(core, own, pair, out):
    c = core[0]

    def step(j, carry):
        rays = pl.ds(pl.multiple_of(256 * j, 256), 256)
        out[j, c] = own[rays, :].T
        out[j, 1 - c] = pair[rays, :].T
        return carry

    lax.fori_loop(0, 8, step, 0)


def project_kernel(blocks, pixels, out, cons, image, turned, held, sems):
    halves = [pl.ds(4 * i, 4) for i in range(2)]
    copies = [
        pltpu.make_async_copy(pixels.at[half], held.at[half], sems.at[i])
        for i, half in enumerate(halves)
    ]
    for copy in copies:
        copy.start()
    for z in range(4):
        for x in range(8):
            got = blocks[pl.ds(z * 8 + x, 16, stride=32), :]
            cons[z * 8 + x] = got
            image[16 * z : 16 * z + 16, 128 * x : 128 * x + 128] = got.astype(BF16)
    for j in range(8):
        if j % 4 == 0:
            copies[j // 4].wait()
        got = jnp.dot(image[:, 0:512], held[j, 0], preferred_element_type=F32)
        got = got + jnp.dot(image[:, 512:1024], held[j, 1], preferred_element_type=F32)
        for z in range(4):
            for n in range(2):
                turned[2 * (j % 4) + n, pl.ds(z * 2 + j // 4, 16, stride=8), :] = got[
                    16 * z : 16 * z + 16, 128 * n : 128 * n + 128
                ]
    for n in range(8):
        lanes = slice(128 * n, 128 * n + 128)
        for t in range(16):
            out[t, :, lanes] = turned[n, 8 * t : 8 * t + 8].astype(BF16)


def misfit_kernel(parts, measured, out):
    total = parts[0].astype(F32)
    for t in range(1, 16):
        total = total + parts[t].astype(F32)
    misfit = (total - measured[...]).astype(BF16)
    for t in range(16):
        out[t] = misfit


def far_kernel(core, misfit, pair, cons, far, rows, turned, held, sems):
    copies = [
        pltpu.make_async_copy(pair.at[pl.ds(512 * j, 512)], held.at[j], sems.at[j])
        for j in range(4)
    ]
    for copy in copies:
        copy.start()
    for n in range(8):
        for t in range(16):
            turned[n, 8 * t : 8 * t + 8] = misfit[t, :, 128 * n : 128 * n + 128].astype(F32)
    for z in range(4):
        for half in range(2):
            for n in range(8):
                rows[16 * z : 16 * z + 16, 1024 * half + 128 * n : 1024 * half + 128 * n + 128] = (
                    turned[n, pl.ds(z * 2 + half, 16, stride=8), :].astype(BF16)
                )
    got = jnp.zeros((64, 512), F32)
    for j in range(4):
        copies[j].wait()
        left = rows[:, 512 * j : 512 * j + 512]
        got = got + jnp.dot(left, held[j], preferred_element_type=F32)
    stepped(1 - core[0], cons, got, far)


def stepped(c, cons, gradient, out):
    for z in range(4):
        for x in range(4):
            at = (slice(16 * z, 16 * z + 16), slice(128 * x, 128 * x + 128))
            out[at] = cons[z * 8 + x + 4 * c] - gradient[at]


def near_kernel(core, rows, own, cons, near):
    got = jnp.dot(rows[...], own[...], preferred_element_type=F32)
    stepped(core[0], cons, got, near)


def merge_kernel(core, near, far, out, turned):
    def write(parity, rows):
        for z in range(4):
            for x in range(4):
                turned[x, pl.ds(4 * parity + z, 16, stride=8), :] = rows[
                    16 * z : 16 * z + 16, 128 * x : 128 * x + 128
                ]

    @pl.when(core[0] == 0)
    def _():
        write(0, near)
        write(1, far)

    @pl.when(core[0] == 1)
    def _():
        write(1, near)
        write(0, far)

    for x in range(4):
        for t in range(32):
            out[t, :, 128 * x : 128 * x + 128] = turned[x, 4 * t : 4 * t + 4]


def shards(volume, lift_weights, lift_bias, mix_weights, out_weights, projector, measured):
    core = lax.axis_index("c").reshape(1)
    parity = (lax.axis_index("space") & 1).reshape(1)
    coarse = volume[0].astype(BF16)
    near = lax.ppermute(coarse, "c", SWAP)
    up = [(2 * i + 1, 2 * i + 2) for i in range(15)]
    next_ = lax.ppermute(coarse, ("q", "c"), up + [(j, i) for i, j in up])
    pair = lax.ppermute(projector, "c", SWAP)

    a1, a2, a3 = call(
        weights_kernel,
        (shaped((3, 512, 256), BF16), shaped((3, 256, 256), BF16), shaped((3, 256, 128), F32)),
        specs=[VM] * 2,
        flops=10**8,
        nbytes=1 << 20,
    )(
        jnp.concatenate([mix_weights, lift_weights.transpose(0, 2, 1)], axis=1),
        jnp.stack([lift_bias, out_weights.astype(F32)]),
    )
    planes, plane = shaped((3, 6, 3, 144, 128), F32), shaped((3, 128, 128), BF16)
    s, to_near, to_next = call(
        spread_kernel, (planes, plane, plane), specs=[SM] * 2 + [VM] * 3, nbytes=8 << 20
    )(core, parity, coarse, near, next_)
    z_near = lax.ppermute(to_near, "space", [(i, i ^ 1) for i in range(8)])
    up = [(2 * i + 1, 2 * i + 2) for i in range(3)]
    z_next = lax.ppermute(to_next, "space", up + [(j, i) for i, j in up])

    blocks = shaped((16, 4, 8, 128), F32)
    xy = call(xy_kernel, blocks, specs=[VM] * 4, flops=12 * 10**9, nbytes=1 << 20)(s, a1, a2, a3)
    consensus, _ = call(
        rest_kernel,
        (blocks, planes),
        specs=[SM] * 2 + [VM] * 8,
        flops=24 * 10**9,
        nbytes=1 << 20,
        aliases={9: 1},
    )(core, parity, volume[0], z_near, z_next, xy, a1, a2, a3, s)
    frames = lax.all_to_all(
        consensus.reshape(16, 32, 128), "q", split_axis=0, concat_axis=0, tiled=True
    )
    pixels = call(
        transpose_kernel,
        shaped((8, 2, 512, 256), BF16),
        specs=[SM, VM, VM],
        nbytes=8 << 20,
    )(core, projector, pair)

    partial, cons = call(
        project_kernel,
        (shaped((16, 8, 1024), BF16), shaped((32, 16, 128), F32)),
        [
            pltpu.VMEM((64, 1024), BF16),
            pltpu.VMEM((8, 128, 128), F32),
            pltpu.VMEM((8, 2, 512, 256), BF16),
            pltpu.SemaphoreType.DMA((2,)),
        ],
        [VM, HB],
        flops=3 * 10**8,
        nbytes=5 << 20,
        vmem=52,
    )(frames.reshape(512, 128), pixels)
    parts = lax.all_to_all(partial, "q", split_axis=0, concat_axis=0, tiled=True)
    misfit = call(misfit_kernel, shaped((16, 8, 1024), BF16), specs=[VM] * 2)(
        parts, measured.reshape(8, 1024)
    )
    misfit = lax.all_to_all(misfit, "q", split_axis=0, concat_axis=0, tiled=True)
    far, rows = call(
        far_kernel,
        (shaped((64, 512), F32), shaped((64, 2048), BF16)),
        [
            pltpu.VMEM((8, 128, 128), F32),
            pltpu.VMEM((4, 512, 512), BF16),
            pltpu.SemaphoreType.DMA((4,)),
        ],
        [SM, VM, HB, VM],
        flops=15 * 10**7,
        nbytes=3 << 20,
    )(core, misfit, pair, cons)
    far = lax.ppermute(far, "c", SWAP)
    near = call(
        near_kernel,
        shaped((64, 512), F32),
        specs=[SM] + [VM] * 3,
        flops=15 * 10**7,
        nbytes=3 << 20,
    )(core, rows, projector, cons)
    return call(
        merge_kernel,
        shaped((32, 4, 512), F32),
        [pltpu.VMEM((4, 128, 128), F32)],
        [SM] + [VM] * 2,
    )(core, near, far)


def solution(mesh):
    fine = Mesh(mesh.devices.reshape(8, 16, 2), ("space", "q", "c"))
    tm = ("q", "c")
    placed = (
        P(tm, "space", None, None),
        P(),
        P(),
        P(),
        P(),
        P(None, tm),
        P(tm, "space", None),
    )
    return jax.shard_map(
        shards, mesh=fine, in_specs=placed, out_specs=P(None, "space", tm), check_vma=False
    )
```

```python
import jax
import jax.numpy as jnp
from jax import lax
from jax.experimental import pallas as pl
from jax.experimental.pallas import tpu as pltpu
from jax.sharding import Mesh, PartitionSpec as P

F32, BF16 = jnp.float32, jnp.bfloat16
VM = pl.BlockSpec(memory_space=pltpu.VMEM)
SM = pl.BlockSpec(memory_space=pltpu.SMEM)
HB = pl.BlockSpec(memory_space=pltpu.HBM)
SWAP = [(0, 1), (1, 0)]
NT = (((1,), (1,)), ((), ()))


def call(kernel, outs, scratch=(), specs=None, flops=0, nbytes=0, vmem=24, aliases=None):
    return pl.pallas_call(
        kernel,
        out_shape=outs,
        in_specs=specs,
        out_specs=jax.tree.map(lambda _: VM, outs),
        scratch_shapes=list(scratch),
        input_output_aliases=aliases or {},
        compiler_params=pltpu.CompilerParams(vmem_limit_bytes=vmem << 20),
        cost_estimate=pl.CostEstimate(flops=flops, bytes_accessed=nbytes, transcendentals=0),
    )


def shaped(shape, dtype):
    return jax.ShapeDtypeStruct(shape, dtype)


def iota(shape, dim):
    return lax.broadcasted_iota(jnp.int32, shape, dim)


def weights_kernel(matrices, vectors, a1, a2, a3):
    spread = (iota((256, 64), 0) >> 2 == iota((256, 64), 1)).astype(F32)
    spread_t = (iota((64, 256), 1) >> 2 == iota((64, 256), 0)).astype(F32).astype(BF16)
    taps = (iota((27, 256), 1) >> 3 == iota((27, 256), 0)).astype(F32).astype(BF16)
    row, col = iota((256, 256), 0) & 3, iota((256, 256), 1)
    tap = col >> 3
    spread_b = spread.astype(BF16)

    def column(values):
        return jnp.sum(spread * values, axis=1, keepdims=True)

    for k in range(3):
        full = vectors[0, k : k + 1]
        high = full.astype(BF16).astype(F32)
        mid = (full - high).astype(BF16).astype(F32)
        low = full - high - mid
        base = lax.dot_general(spread_b, matrices[k, 64:91], NT, preferred_element_type=F32).astype(BF16)
        base = jnp.dot(base, taps, preferred_element_type=F32)
        for at, part in ((27, high), (28, mid), (29, low)):
            base = jnp.where(tap == at, column(part), base)
        for half in range(2):
            a1[k, half * 256 : half * 256 + 256] = jnp.where(
                row + 4 * half == (col & 7), base, 0.0
            ).astype(BF16)
        mixed = jnp.dot(spread_b, matrices[k, 0:64], preferred_element_type=F32).astype(BF16)
        mixed = jnp.dot(mixed, spread_t, preferred_element_type=F32)
        a2[k] = jnp.where(row == (col & 3), mixed, 0.0).astype(BF16)
        a3[k] = jnp.broadcast_to(column(vectors[1, k : k + 1]), (256, 128))


def spread_plane(s, t, z, plane):
    zero = jnp.zeros((8, 128), F32)
    lane = iota((8, 128), 1)
    for dy in range(3):
        s[t, z, dy, 0:8] = zero
        s[t, z, dy, 136:144] = zero
    for j in range(8):
        pair = plane[16 * j : 16 * j + 16].astype(F32)
        for i in range(2):
            v = pair[8 * i : 8 * i + 8]
            at = slice(16 * j + 8 * i + 8, 16 * j + 8 * i + 16)
            s[t, z, 0, at] = jnp.where(lane == 0, 0.0, pltpu.roll(v, 1, 1))
            s[t, z, 1, at] = v
            s[t, z, 2, at] = jnp.where(lane == 127, 0.0, pltpu.roll(v, 127, 1))


def spread_kernel(core, parity, mine, near, next_, s, to_near, to_next):
    c, odd = core[0], parity[0]
    for i, ref in enumerate((mine, near, next_)):
        to_near[i] = ref[3 - 3 * odd]
        to_next[i] = ref[3 * odd]

    def step(z, carry):
        spread_plane(s, 1, z + 1, mine[z])
        spread_plane(s, 2 - 2 * c, z + 1, near[z])
        spread_plane(s, 2 * c, z + 1, next_[z])
        return carry

    lax.fori_loop(0, 4, step, 0)


OFFSETS = (
    [(dt, 1, db, da) for dt in range(3) for da in range(3) for db in range(3)],
    [(dt, db, da, 1) for dt in range(3) for da in range(3) for db in range(3)],
    [(dt, da, 1, db) for dt in range(3) for da in range(3) for db in range(3)],
)


def corrected(s, a1, a2, a3, which, z, block):
    rows = []
    for dt, dz, dy, dx in OFFSETS[which]:
        at = 7 + dx + 16 * block
        rows.append(
            jnp.concatenate(
                [s[dt, z + dz, dy, at : at + 8], s[dt, z + dz, dy, at + 8 : at + 16]], axis=1
            )
        )
    rows.append(jnp.ones((24, 256), F32))
    rows.append(jnp.zeros((16, 256), F32))
    taps = jnp.concatenate(rows, axis=0).astype(BF16)
    first = jnp.dot(a1[which], taps, preferred_element_type=F32)
    first = jnp.maximum(first, 0.0).astype(BF16)
    w = a3[which]
    w = jnp.concatenate([w, w], axis=1)
    sums = []
    for half in range(2):
        second = jnp.dot(
            a2[which], first[half * 256 : half * 256 + 256], preferred_element_type=F32
        )
        second = jnp.maximum(second, 0.0) * w
        total = jnp.sum(second.reshape(32, 8, 256), axis=0)
        sums.append(total + pltpu.roll(total, 4, 0))
    return jnp.where(iota((8, 256), 0) < 4, sums[0], sums[1])


def xy_kernel(s, a1, a2, a3, out):
    for z in range(4):
        for block in range(8):
            got = corrected(s, a1, a2, a3, 0, z, block)
            out[2 * block, z] = got[:, :128]
            out[2 * block + 1, z] = got[:, 128:]


def rest_kernel(core, parity, vol, near, next_, xy, a1, a2, a3, s_in, cons, s):
    c, odd = core[0], parity[0]
    for i, t in enumerate((1, 2 - 2 * c, 2 * c)):
        spread_plane(s, t, 5 - 5 * odd, near[i])
        spread_plane(s, t, 5 * odd, next_[i])

    for z in range(4):
        for block in range(8):
            got = corrected(s, a1, a2, a3, 1, z, block)
            got = got + corrected(s, a1, a2, a3, 2, z, block)
            for j in range(2):
                at = 2 * block + j
                total = xy[at, z] + got[:, 128 * j : 128 * j + 128]
                cons[at, z] = vol[z, 8 * at : 8 * at + 8] + total / 3.0


def transpose_kernel(core, own, pair, out):
    c = core[0]

    def step(j, carry):
        rays = pl.ds(pl.multiple_of(256 * j, 256), 256)
        out[j, c] = own[rays, :].T
        out[j, 1 - c] = pair[rays, :].T
        return carry

    lax.fori_loop(0, 8, step, 0)


def project_kernel(blocks, pixels, out, cons, image, turned, held, sems):
    halves = [pl.ds(4 * i, 4) for i in range(2)]
    copies = [
        pltpu.make_async_copy(pixels.at[half], held.at[half], sems.at[i])
        for i, half in enumerate(halves)
    ]
    for copy in copies:
        copy.start()
    for z in range(4):
        for x in range(8):
            got = blocks[pl.ds(z * 8 + x, 16, stride=32), :]
            cons[z * 8 + x] = got
            image[16 * z : 16 * z + 16, 128 * x : 128 * x + 128] = got.astype(BF16)
    for j in range(8):
        if j % 4 == 0:
            copies[j // 4].wait()
        got = jnp.dot(image[:, 0:512], held[j, 0], preferred_element_type=F32)
        got = got + jnp.dot(image[:, 512:1024], held[j, 1], preferred_element_type=F32)
        for z in range(4):
            for n in range(2):
                turned[2 * (j % 4) + n, pl.ds(z * 2 + j // 4, 16, stride=8), :] = got[
                    16 * z : 16 * z + 16, 128 * n : 128 * n + 128
                ]
    for n in range(8):
        lanes = slice(128 * n, 128 * n + 128)
        for t in range(16):
            out[t, :, lanes] = turned[n, 8 * t : 8 * t + 8].astype(BF16)


def misfit_kernel(parts, measured, out):
    total = parts[0].astype(F32)
    for t in range(1, 16):
        total = total + parts[t].astype(F32)
    misfit = (total - measured[...]).astype(BF16)
    for t in range(16):
        out[t] = misfit


def far_kernel(core, misfit, pair, cons, far, rows, turned, held, sems):
    copies = [
        pltpu.make_async_copy(pair.at[pl.ds(1024 * j, 1024)], held.at[j], sems.at[j])
        for j in range(2)
    ]
    for copy in copies:
        copy.start()
    for n in range(8):
        for t in range(16):
            turned[n, 8 * t : 8 * t + 8] = misfit[t, :, 128 * n : 128 * n + 128].astype(F32)
    for z in range(4):
        for half in range(2):
            for n in range(8):
                rows[16 * z : 16 * z + 16, 1024 * half + 128 * n : 1024 * half + 128 * n + 128] = (
                    turned[n, pl.ds(z * 2 + half, 16, stride=8), :].astype(BF16)
                )
    got = jnp.zeros((64, 512), F32)
    for j in range(2):
        copies[j].wait()
        left = rows[:, 1024 * j : 1024 * j + 1024]
        got = got + jnp.dot(left, held[j], preferred_element_type=F32)
    stepped(1 - core[0], cons, got, far)


def stepped(c, cons, gradient, out):
    for z in range(4):
        for x in range(4):
            at = (slice(16 * z, 16 * z + 16), slice(128 * x, 128 * x + 128))
            out[at] = cons[z * 8 + x + 4 * c] - gradient[at]


def near_kernel(core, rows, own, cons, near):
    got = jnp.dot(rows[...], own[...], preferred_element_type=F32)
    stepped(core[0], cons, got, near)


def merge_kernel(core, near, far, out, turned):
    def write(parity, rows):
        for z in range(4):
            for x in range(4):
                turned[x, pl.ds(4 * parity + z, 16, stride=8), :] = rows[
                    16 * z : 16 * z + 16, 128 * x : 128 * x + 128
                ]

    @pl.when(core[0] == 0)
    def _():
        write(0, near)
        write(1, far)

    @pl.when(core[0] == 1)
    def _():
        write(1, near)
        write(0, far)

    for x in range(4):
        for t in range(32):
            out[t, :, 128 * x : 128 * x + 128] = turned[x, 4 * t : 4 * t + 4]


def shards(volume, lift_weights, lift_bias, mix_weights, out_weights, projector, measured):
    core = lax.axis_index("c").reshape(1)
    parity = (lax.axis_index("space") & 1).reshape(1)
    coarse = volume[0].astype(BF16)
    near = lax.ppermute(coarse, "c", SWAP)
    up = [(2 * i + 1, 2 * i + 2) for i in range(15)]
    next_ = lax.ppermute(coarse, ("q", "c"), up + [(j, i) for i, j in up])
    pair = lax.ppermute(projector, "c", SWAP)

    a1, a2, a3 = call(
        weights_kernel,
        (shaped((3, 512, 256), BF16), shaped((3, 256, 256), BF16), shaped((3, 256, 128), F32)),
        specs=[VM] * 2,
        flops=10**8,
        nbytes=1 << 20,
    )(
        jnp.concatenate([mix_weights, lift_weights.transpose(0, 2, 1)], axis=1),
        jnp.stack([lift_bias, out_weights.astype(F32)]),
    )
    planes, plane = shaped((3, 6, 3, 144, 128), F32), shaped((3, 128, 128), BF16)
    s, to_near, to_next = call(
        spread_kernel, (planes, plane, plane), specs=[SM] * 2 + [VM] * 3, nbytes=8 << 20
    )(core, parity, coarse, near, next_)
    z_near = lax.ppermute(to_near, "space", [(i, i ^ 1) for i in range(8)])
    up = [(2 * i + 1, 2 * i + 2) for i in range(3)]
    z_next = lax.ppermute(to_next, "space", up + [(j, i) for i, j in up])

    blocks = shaped((16, 4, 8, 128), F32)
    xy = call(xy_kernel, blocks, specs=[VM] * 4, flops=12 * 10**9, nbytes=1 << 20)(s, a1, a2, a3)
    consensus, _ = call(
        rest_kernel,
        (blocks, planes),
        specs=[SM] * 2 + [VM] * 8,
        flops=24 * 10**9,
        nbytes=1 << 20,
        aliases={9: 1},
    )(core, parity, volume[0], z_near, z_next, xy, a1, a2, a3, s)
    frames = lax.all_to_all(
        consensus.reshape(16, 32, 128), "q", split_axis=0, concat_axis=0, tiled=True
    )
    pixels = call(
        transpose_kernel,
        shaped((8, 2, 512, 256), BF16),
        specs=[SM, VM, VM],
        nbytes=8 << 20,
    )(core, projector, pair)

    partial, cons = call(
        project_kernel,
        (shaped((16, 8, 1024), BF16), shaped((32, 16, 128), F32)),
        [
            pltpu.VMEM((64, 1024), BF16),
            pltpu.VMEM((8, 128, 128), F32),
            pltpu.VMEM((8, 2, 512, 256), BF16),
            pltpu.SemaphoreType.DMA((2,)),
        ],
        [VM, HB],
        flops=3 * 10**8,
        nbytes=5 << 20,
        vmem=52,
    )(frames.reshape(512, 128), pixels)
    parts = lax.all_to_all(partial, "q", split_axis=0, concat_axis=0, tiled=True)
    misfit = call(misfit_kernel, shaped((16, 8, 1024), BF16), specs=[VM] * 2)(
        parts, measured.reshape(8, 1024)
    )
    misfit = lax.all_to_all(misfit, "q", split_axis=0, concat_axis=0, tiled=True)
    far, rows = call(
        far_kernel,
        (shaped((64, 512), F32), shaped((64, 2048), BF16)),
        [
            pltpu.VMEM((8, 128, 128), F32),
            pltpu.VMEM((2, 1024, 512), BF16),
            pltpu.SemaphoreType.DMA((2,)),
        ],
        [SM, VM, HB, VM],
        flops=15 * 10**7,
        nbytes=3 << 20,
    )(core, misfit, pair, cons)
    far = lax.ppermute(far, "c", SWAP)
    near = call(
        near_kernel,
        shaped((64, 512), F32),
        specs=[SM] + [VM] * 3,
        flops=15 * 10**7,
        nbytes=3 << 20,
    )(core, rows, projector, cons)
    return call(
        merge_kernel,
        shaped((32, 4, 512), F32),
        [pltpu.VMEM((4, 128, 128), F32)],
        [SM] + [VM] * 2,
    )(core, near, far)


def solution(mesh):
    fine = Mesh(mesh.devices.reshape(8, 16, 2), ("space", "q", "c"))
    tm = ("q", "c")
    placed = (
        P(tm, "space", None, None),
        P(),
        P(),
        P(),
        P(),
        P(None, tm),
        P(tm, "space", None),
    )
    return jax.shard_map(
        shards, mesh=fine, in_specs=placed, out_specs=P(None, "space", tm), check_vma=False
    )
```
